32 devices in a mesh: dom: 8 (over z, y), bin: 4 (over x, core).
Axes of the slice: x: 2, y: 2, z: 4, core: 2. Of those that a mesh axis runs over, the one named last changes fastest.
Arguments:
- field_in: float32 [8, 131072], P(None, ('dom', 'bin')), may hold values from -6 to 6
- heading_in: float32 [3, 131072], P(None, ('dom', 'bin')), may hold values from -3 to 3
- launch_domain: int32 [131072, 1], P(('dom', 'bin')), may hold values from 0 to 7; in each aligned block of 4096 rows (0 to 4095, 4096 to 8191, ...) at most 1024 rows name the same one
- hop_domain: int32 [3, 131072, 1], P(None, ('dom', 'bin')), may hold values from 0 to 7; in each aligned block of 4096 rows (0 to 4095, 4096 to 8191, ..., all dimensions but the last counted through in order) at most 1024 rows name the same one
- hit_facet: int32 [4, 131072], P(None, ('dom', 'bin')), may hold values from 0 to 8191
- path_phase: float32 [4, 131072], P(None, ('dom', 'bin')), may hold values from -3.140625 to 3.140625
- facet_polar: float32 [65536], P('dom'), may hold values from -3.140625 to 3.140625
- facet_azimuth: float32 [65536], P('dom'), may hold values from -3.140625 to 3.140625
- facet_tilt: float32 [65536], P('dom'), may hold values from -3.140625 to 3.140625
- surface_resistance: float32 [65536], P('dom'), may hold values from 0.2 to 5
- surface_reactance: float32 [65536], P('dom'), may hold values from -1 to 1
- kernel: bfloat16 [2, 65536, 1024], P(None, ('dom', 'bin')), may hold values from -0.005859375 to 0.005859375
Outputs:
- far_field: float32 [8, 1024], P(None, ('dom', 'bin'))
- exit_field: float32 [8, 131072], P(None, ('dom', 'bin'))
The draws below stay inside these ranges and needn't reach their ends.
Inputs may be any that keep to these rules, and one draw needn't show every extreme that they name: `launch_domain`: among the 4096 tubes launched from one device (aligned blocks of the tube dimension), each domain is named at most 1024 times in each bounce, and exactly 1024 times by some domain in some blocks. `hop_domain`: among the 4096 tubes launched from one device, each domain is named at most 1024 times in each bounce, and exactly 1024 times by some domain in some blocks.
All inputs are finite; a program needn't handle non-finite values.
Results may differ from the reference program's by a relative error of at most 0.0029.
Values sent between devices are 32-bit elements; how exact they have to be, the bound alone decides.
No kernel may reach another device: no remote copies, remote signals or barrier semaphores. Data moves between devices by JAX's collectives and lax.ppermute only.
A program may use at most 128 MiB of HBM per device.

```python
import math
import jax
import jax.numpy as jnp
import numpy as np

TUBES_DEV = 4096
BOUNCES = 4
FAC = 8192
BINS = 1024
TUBES = 131072
FACETS = 65536
CAP = 1024
N_DOM = 8


def touch_ends(drawn, stream_key, least, top_value):
    longest = drawn.shape.index(max(drawn.shape))
    spots = []
    for shift in (0, 1):
        where = [jax.random.randint(jax.random.fold_in(stream_key, axis), (), 0, length) for axis, length in enumerate(drawn.shape)]
        where[longest] = (where[longest] + shift) % drawn.shape[longest]
        spots.append(tuple(where))
    return drawn.at[spots[0]].set(least).at[spots[1]].set(top_value)


def with_spikes(drawn, own_key, source, target, blocks, factor):
    owner, partner = [(jnp.arange(drawn.shape[axis_at]) // (drawn.shape[axis_at] // blocks)).reshape([-1 if axis == axis_at else 1 for axis in range(drawn.ndim)]) for axis_at in (source, target)]
    chosen = jax.random.permutation(own_key, blocks)[partner]
    strong = (owner == chosen) | (owner == (partner + blocks // 2) % blocks)
    return jnp.where(strong, factor * drawn, drawn)


def steps_of(key, extent, shards, smallest, largest):
    gain, own = 1.0, jax.random.fold_in(key, 6)
    for dim, parts in shards:
        steps = jnp.exp(jax.random.uniform(jax.random.fold_in(own, dim), (parts,), jnp.float32, smallest / len(shards), largest / len(shards)))
        gain = gain * jnp.repeat(steps, extent[dim] // parts).reshape([-1 if axis == dim else 1 for axis in range(len(extent))])
    return gain


def deal_out(key, own, number, rows, count, top, bound, skew):
    ranking = jax.random.permutation(key, count)
    packed, usual = portions_of(count, rows * top, bound, skew, True), portions_of(count, rows * top, bound, skew, False)
    places = jnp.arange(count)

    def named(sizes, offset_by):
        used = int((sizes > 0).sum())
        fixed = max(1, used // 4)
        shifted = fixed + (places - fixed + offset_by * (used - fixed)) % max(1, count - fixed)
        return jnp.zeros((count,), jnp.int32).at[ranking[jnp.where(places < fixed, places, shifted)]].set(jnp.asarray(sizes, jnp.int32))

    sizes = jnp.where(number % 4 == 0, named(packed, number // 4), named(usual, number - number // 4 - 1))
    mixed = jax.random.permutation(jax.random.fold_in(own, 3), count)
    donor, sink = mixed[0:count // 2 * 2:2], mixed[1:count // 2 * 2:2]
    margin = jnp.minimum(sizes[donor] - 1, bound - sizes[sink]) // 2
    margin = jnp.where((donor == ranking[0]) | (sink == ranking[0]) | (sizes[sink] == 0), 0, jnp.maximum(margin, 0))
    shifted = jax.random.randint(jax.random.fold_in(own, 4), (count // 2,), 0, 1 << 20) % (margin + 1)
    sizes = sizes.at[donor].add(-shifted).at[sink].add(shifted)
    labels = jnp.searchsorted(jnp.cumsum(sizes), jnp.arange(rows * top), side="right").astype(jnp.int32)
    table = labels.reshape(top, rows).T
    table = table[jax.random.permutation(jax.random.fold_in(own, 1), rows)]
    offset_by = jax.random.randint(jax.random.fold_in(own, 2), (rows, 1), 0, top)
    return jnp.take_along_axis(table, (jnp.arange(top)[None, :] + offset_by) % top, axis=1)


def portions_of(number_of, total, reach, slope, full):
    weights = [(1 << 20) // math.isqrt(standing ** slope) + 1 for standing in range(1, number_of + 1)]
    largest = reach if full else min(reach, max(-(-total // number_of), total * weights[0] // sum(weights)))
    least = 1 if total - largest >= number_of - 1 else 0
    counts, rest = [largest] + [least] * (number_of - 1), total - largest - least * (number_of - 1)
    while rest > 0:
        free = [i for i in range(1, number_of) if counts[i] < largest] or [i for i in range(1, number_of) if counts[i] < reach]
        whole, budget = sum([weights[i] for i in free]), rest
        for i in free:
            addition = min(reach - counts[i], max(1, budget * weights[i] // whole), rest)
            counts[i] = counts[i] + addition
            rest = rest - addition
    return np.array(counts)


def noise(key, dims, width, reach, split=(), dtype=jnp.bfloat16):
    values = width * jax.random.normal(key, dims, jnp.float32)
    if split:
        values = values * steps_of(key, dims, split, -0.22, 0.18)
    return jnp.clip(values, -reach, reach).astype(dtype)


def bell_draw_with(rng, extent, scale, most, split, heavy, held_as=jnp.bfloat16):
    values = scale * jax.random.normal(rng, extent, jnp.float32)
    if split:
        values = values * steps_of(rng, extent, split, -0.22, 0.18)
    return jnp.clip(with_spikes(values, jax.random.fold_in(rng, 3), *heavy), -most, most).astype(held_as)


def setup_inputs(seed: int = 0) -> dict:
    seeds = jax.random.split(jax.random.key(seed), 13)
    field_in = noise(seeds[0], (8, TUBES), 1.0, 6.0, ((1, 32),), jnp.float32)
    heading_in = noise(seeds[1], (3, TUBES), 0.6, 3.0, ((1, 32),), jnp.float32)
    launch_domain_keys = jax.random.split(jax.random.fold_in(seeds[2], 1), TUBES // TUBES_DEV)
    launch_domain_turns = jax.random.permutation(jax.random.fold_in(seeds[2], 3), TUBES // TUBES_DEV)
    launch_domain = jax.vmap(lambda own, number: deal_out(jax.random.fold_in(seeds[2], 2), own, number, TUBES_DEV, N_DOM, 1, CAP, 2))(launch_domain_keys, launch_domain_turns).reshape((TUBES, 1))
    hop_domain_keys = jax.random.split(jax.random.fold_in(seeds[3], 1), (BOUNCES - 1) * TUBES // TUBES_DEV)
    hop_domain_turns = jax.random.permutation(jax.random.fold_in(seeds[3], 3), (BOUNCES - 1) * TUBES // TUBES_DEV)
    hop_domain = jax.vmap(lambda own, number: deal_out(jax.random.fold_in(seeds[3], 2), own, number, TUBES_DEV, N_DOM, 1, CAP, 2))(hop_domain_keys, hop_domain_turns).reshape((BOUNCES - 1, TUBES, 1))
    hit_facet = touch_ends(jax.random.randint(seeds[4], (BOUNCES, TUBES), 0, FAC), jax.random.fold_in(seeds[4], 1), 0, FAC - 1).astype(jnp.int32)
    path_phase = jnp.clip(jax.random.uniform(seeds[5], (BOUNCES, TUBES), jnp.float32, -3.140625, 3.140625), -3.140625, 3.140625)
    facet_polar = jnp.clip(jax.random.uniform(seeds[6], (FACETS,), jnp.float32, -3.140625, 3.140625), -3.140625, 3.140625)
    facet_azimuth = jnp.clip(jax.random.uniform(seeds[7], (FACETS,), jnp.float32, -3.140625, 3.140625), -3.140625, 3.140625)
    facet_tilt = jnp.clip(jax.random.uniform(seeds[8], (FACETS,), jnp.float32, -3.140625, 3.140625), -3.140625, 3.140625)
    surface_resistance = jnp.clip(jnp.exp(math.log(5.0) - 3.218876 * jax.random.uniform(seeds[9], (FACETS,), jnp.float32) ** steps_of(seeds[9], (FACETS,), ((0, 8),), -0.2, 0.2)), 0.2, 5.0)
    surface_reactance = jnp.clip(jax.random.uniform(seeds[10], (FACETS,), jnp.float32, -1.0, 1.0) * steps_of(seeds[10], (FACETS,), ((0, 8),), -0.4, 0.0), -1.0, 1.0)
    kernel = bell_draw_with(seeds[11], (2, FACETS, BINS), (64 * FACETS) ** -0.5, 0.005859375, ((1, 32),), (1, 2, 32, 2.75))
    return {"field_in": field_in, "heading_in": heading_in, "launch_domain": launch_domain, "hop_domain": hop_domain, "hit_facet": hit_facet, "path_phase": path_phase, "facet_polar": facet_polar, "facet_azimuth": facet_azimuth, "facet_tilt": facet_tilt, "surface_resistance": surface_resistance, "surface_reactance": surface_reactance, "kernel": kernel}


def facet_frame(polar_angle, azimuth, tilt_angle, resistance, reactance):
    return jnp.stack([jnp.sin(polar_angle) * jnp.cos(azimuth), jnp.sin(polar_angle) * jnp.sin(azimuth), jnp.cos(polar_angle), resistance, reactance, jnp.cos(tilt_angle), jnp.sin(tilt_angle)], axis=0)


def divide(top_real, top_imag, low_real, low_imag):
    modulus = low_real * low_real + low_imag * low_imag
    return (top_real * low_real + top_imag * low_imag) / modulus, (top_imag * low_real - top_real * low_imag) / modulus


def turn_phase(tube_field, phase_angle):
    phase_cos = jnp.cos(phase_angle)
    phase_sin = jnp.sin(phase_angle)
    return jnp.concatenate([phase_cos * tube_field[0:4] - phase_sin * tube_field[4:8], phase_sin * tube_field[0:4] + phase_cos * tube_field[4:8]], axis=0)


def reflect(tube_field, heading, facet_rows):
    normal = facet_rows[0:3]
    incidence = jnp.sum(heading * normal, axis=0)
    cosine = jnp.abs(incidence)
    eta_real = facet_rows[3]
    eta_imag = facet_rows[4]
    tilt_cos = facet_rows[5]
    tilt_sin = facet_rows[6]
    te_real, te_imag = divide(cosine - eta_real, -eta_imag, cosine + eta_real, eta_imag)
    tm_real, tm_imag = divide(eta_real * cosine - 1.0, eta_imag * cosine, eta_real * cosine + 1.0, eta_imag * cosine)
    upper_real = tilt_cos * tube_field[0:2] + tilt_sin * tube_field[2:4]
    lower_real = tilt_cos * tube_field[2:4] - tilt_sin * tube_field[0:2]
    upper_imag = tilt_cos * tube_field[4:6] + tilt_sin * tube_field[6:8]
    lower_imag = tilt_cos * tube_field[6:8] - tilt_sin * tube_field[4:6]
    result = jnp.concatenate([te_real * upper_real - te_imag * upper_imag, tm_real * lower_real - tm_imag * lower_imag, te_real * upper_imag + te_imag * upper_real, tm_real * lower_imag + tm_imag * lower_real], axis=0)
    turned = heading - 2.0 * incidence * normal
    return result, turned


def reference(field_in, heading_in, launch_domain, hop_domain, hit_facet, path_phase, facet_polar, facet_azimuth, facet_tilt, surface_resistance, surface_reactance, kernel):
    frame_all = facet_frame(facet_polar, facet_azimuth, facet_tilt, surface_resistance, surface_reactance)
    tube_field = field_in
    heading = heading_in
    facet_sums = jnp.zeros((8, FACETS), jnp.float32)
    for bounce in range(BOUNCES):
        if bounce == 0:
            target = launch_domain[:, 0].astype(jnp.int32)
        else:
            target = hop_domain[bounce - 1, :, 0].astype(jnp.int32)
        global_facet = (target * FAC + hit_facet[bounce].astype(jnp.int32)).astype(jnp.int32)
        phased = turn_phase(tube_field, path_phase[bounce])
        facet_rows = jnp.take(frame_all, global_facet, axis=1)
        tube_field, heading = reflect(phased, heading, facet_rows)
        facet_sums = facet_sums.at[:, global_facet].add(tube_field)
    rounded = facet_sums.astype(jnp.bfloat16)
    real_part = jnp.dot(rounded, kernel[0], preferred_element_type=jnp.float32)
    imag_part = jnp.dot(rounded, kernel[1], preferred_element_type=jnp.float32)
    far_field = jnp.concatenate([real_part[0:4] - imag_part[4:8], imag_part[0:4] + real_part[4:8]], axis=0)
    return far_field, tube_field
```

```python
import functools

import jax
import jax.numpy as jnp
from jax import lax
from jax.experimental import pallas as pl
from jax.experimental.pallas import tpu as pltpu
from jax.sharding import PartitionSpec as P

BOUNCES = 4
LANES = 128
VALUES = 8
GROUPS = LANES // VALUES
VMEM = pl.BlockSpec(memory_space=pltpu.VMEM)
SMEM = pl.BlockSpec(memory_space=pltpu.SMEM)
ANY = pl.BlockSpec(memory_space=pl.ANY)
F32 = jnp.float32


def bits_of(count):
    assert count & (count - 1) == 0
    return count.bit_length() - 1


def sum_phases(bits):
    phases = [[0]]
    rest = list(range(1, bits))
    while rest:
        phases.append(rest[:2])
        rest = rest[2:]
    return phases


def spread(digit, phase):
    return sum(((digit >> place) & 1) << bit for place, bit in enumerate(phase))


def place_of(offset, phases):
    place = 0
    for phase in phases:
        for bit in reversed(phase):
            place = place * 2 + ((offset >> bit) & 1)
    return place


def send(value, mask, axes, count):
    return lax.ppermute(value, axes, [(i, i ^ mask) for i in range(count)])


def sine_cosine(angle):
    turns = jnp.floor(angle * 0.6366197723675814 + 0.5)
    rest = angle - turns * 1.5703125
    rest = rest - turns * 4.837512969970703e-4
    rest = rest - turns * 7.54978995489188e-8
    square = rest * rest
    sine = rest + rest * square * (
        -1.6666654611e-1 + square * (8.3321608736e-3 - square * 1.9515295891e-4)
    )
    cosine = 1.0 - 0.5 * square + square * square * (
        4.166664568298827e-2 + square * (-1.388731625493765e-3 + square * 2.443315711809948e-5)
    )
    quarter = turns.astype(jnp.int32)
    odd = (quarter & 1) == 1
    first = jnp.where(odd, cosine, sine)
    second = jnp.where(odd, sine, cosine)
    return (
        jnp.where((quarter & 2) == 2, -first, first),
        jnp.where(((quarter + 1) & 2) == 2, -second, second),
    )


def divide(top_real, top_imag, low_real, low_imag):
    scale = 1.0 / (low_real * low_real + low_imag * low_imag)
    return (
        (top_real * low_real + top_imag * low_imag) * scale,
        (top_imag * low_real - top_real * low_imag) * scale,
    )


def bounce_once(field, heading, facet, phase):
    sine, cosine = sine_cosine(phase)
    real = [cosine * field[i] - sine * field[4 + i] for i in range(4)]
    imag = [sine * field[i] + cosine * field[4 + i] for i in range(4)]
    normal = facet[0:3]
    eta_real, eta_imag, tilt_cos, tilt_sin = facet[3:7]
    incidence = heading[0] * normal[0] + heading[1] * normal[1] + heading[2] * normal[2]
    slant = jnp.abs(incidence)
    te_real, te_imag = divide(slant - eta_real, -eta_imag, slant + eta_real, eta_imag)
    tm_real, tm_imag = divide(
        eta_real * slant - 1.0, eta_imag * slant, eta_real * slant + 1.0, eta_imag * slant
    )
    out_real, out_imag = [None] * 4, [None] * 4
    for i in range(2):
        upper_real = tilt_cos * real[i] + tilt_sin * real[2 + i]
        lower_real = tilt_cos * real[2 + i] - tilt_sin * real[i]
        upper_imag = tilt_cos * imag[i] + tilt_sin * imag[2 + i]
        lower_imag = tilt_cos * imag[2 + i] - tilt_sin * imag[i]
        out_real[i] = te_real * upper_real - te_imag * upper_imag
        out_real[2 + i] = tm_real * lower_real - tm_imag * lower_imag
        out_imag[i] = te_real * upper_imag + te_imag * upper_real
        out_imag[2 + i] = tm_real * lower_imag + tm_imag * lower_real
    twice = 2.0 * incidence
    return out_real + out_imag, [heading[k] - twice * normal[k] for k in range(3)]


def trace_kernel(meta, *refs):
    (tubes, pieces, piece_rows, bins, depth, phases, parts, copies, axes) = meta
    rows_ref, group_ref, phase_ref, field_ref, heading_ref = refs[:5]
    piece_refs = refs[5 : 5 + pieces]
    part_refs = refs[5 + pieces : 5 + pieces + parts]
    exit_ref = refs[5 + pieces + parts]
    scratch = refs[6 + pieces + parts :]
    table, frame, wide, turn, flat, arrive, leave = scratch[:7]
    sums = scratch[7:]
    blocks = tubes // LANES
    total = sums[0].shape[0]

    loads = [
        pltpu.make_async_copy(piece_refs[i], table.at[i], arrive.at[i]) for i in range(pieces)
    ]
    for load in loads:
        load.start()

    clear = 256
    zeros = jnp.zeros((clear, LANES), F32)

    def wipe(i, carry):
        for ref in sums:
            ref[pl.ds(pl.multiple_of(i * clear, clear), clear), :] = zeros
        return carry

    lax.fori_loop(0, total // clear, wipe, 0)
    for load in loads:
        load.wait()

    me = lax.axis_index(axes[1])
    low = me & 1
    quarters = bins // 2
    per_quarter = piece_rows // quarters
    steps = depth // LANES

    def build(i, carry):
        polar, azimuth, tilt = table[i, 0], table[i, 1], table[i, 2]
        polar_sin, polar_cos = sine_cosine(polar)
        azimuth_sin, azimuth_cos = sine_cosine(azimuth)
        tilt_sin, tilt_cos = sine_cosine(tilt)
        values = [
            polar_sin * azimuth_cos,
            polar_sin * azimuth_sin,
            polar_cos,
            table[i, 3],
            table[i, 4],
            tilt_cos,
            tilt_sin,
            tilt_sin,
        ]
        for k in range(VALUES):
            frame[k * piece_rows : (k + 1) * piece_rows, :] = values[k]
        half = (i & 1) ^ low
        for quarter in range(quarters):
            owner = half * quarters + quarter
            place = place_of((i >> 1) * bins + (owner ^ me), phases)
            for m in range(steps):
                tall = jnp.concatenate(
                    [
                        frame[
                            pl.ds(quarter * per_quarter + j * steps + m, VALUES, stride=piece_rows),
                            :,
                        ]
                        for j in range(GROUPS)
                    ],
                    axis=0,
                )
                at = pl.multiple_of(place * depth + m * LANES, LANES)
                flat[pl.ds(at, LANES), :] = tall.T
        return carry

    lax.fori_loop(0, pieces, build, 0)

    unroll = 32

    def fetch(i, carry):
        for u in range(unroll):
            hit = i * unroll + u
            wide[pl.ds(hit, 1), :] = flat[pl.ds(rows_ref[hit], 1), :]
        return carry

    lax.fori_loop(0, BOUNCES * tubes // unroll, fetch, 0)

    def spread_in(ref, count):
        for k in range(blocks):
            turn[k * VALUES : k * VALUES + count, :] = ref[:, k * LANES : (k + 1) * LANES]
        return [turn[pl.ds(c, blocks, stride=VALUES), :] for c in range(count)]

    field = spread_in(field_ref, 8)
    heading = spread_in(heading_ref, 3)
    for bounce in range(BOUNCES):

        def pick(k, carry, bounce=bounce):
            at = pl.multiple_of((bounce * blocks + k) * LANES, LANES)
            tall = wide[pl.ds(at, LANES), :].T.reshape(GROUPS, VALUES, LANES)
            group = group_ref[bounce, pl.ds(k, 1), :]
            left = [tall[j] for j in range(GROUPS)]
            level = 0
            while len(left) > 1:
                odd = jnp.broadcast_to((group >> level) & 1, (VALUES, LANES)) == 1
                left = [jnp.where(odd, left[2 * n + 1], left[2 * n]) for n in range(len(left) // 2)]
                level += 1
            turn[pl.ds(pl.multiple_of(k * VALUES, VALUES), VALUES), :] = left[0]
            return carry

        lax.fori_loop(0, blocks, pick, 0)
        facet = [turn[pl.ds(c, blocks, stride=VALUES), :] for c in range(7)]
        field, heading = bounce_once(field, heading, facet, phase_ref[bounce])
        for c in range(VALUES):
            turn[c * blocks : (c + 1) * blocks, :] = field[c]

        def widen(k, carry, bounce=bounce):
            at = pl.multiple_of((bounce * blocks + k) * LANES, LANES)
            own = turn[pl.ds(k, VALUES, stride=blocks), :]
            group = jnp.broadcast_to(group_ref[bounce, pl.ds(k, 1), :], (VALUES, LANES))
            tall = jnp.concatenate([jnp.where(group == j, own, 0.0) for j in range(GROUPS)], axis=0)
            wide[pl.ds(at, LANES), :] = tall.T
            if bounce == BOUNCES - 1:
                exit_ref[:, pl.ds(pl.multiple_of(k * LANES, LANES), LANES)] = own
            return carry

        lax.fori_loop(0, blocks, widen, 0)

    share = BOUNCES * tubes // copies
    inner = 32 // copies

    def add(i, carry):
        for u in range(inner):
            fresh = []
            for c in range(copies):
                hit = c * share + i * inner + u
                row = rows_ref[hit]
                fresh.append((row, sums[c][pl.ds(row, 1), :] + wide[pl.ds(hit, 1), :]))
            for c in range(copies):
                sums[c][pl.ds(fresh[c][0], 1), :] = fresh[c][1]
        return carry

    lax.fori_loop(0, share // inner, add, 0)

    size = total // parts
    outs = []
    for part in range(parts):

        def merge(i, carry, part=part):
            at = pl.ds(pl.multiple_of(part * size + i * LANES, LANES), LANES)
            sums[0][at, :] = functools.reduce(lambda a, b: a + b, [ref[at, :] for ref in sums])
            return carry

        if copies > 1:
            lax.fori_loop(0, size // LANES, merge, 0)
        outs.append(
            pltpu.make_async_copy(
                sums[0].at[pl.ds(part * size, size), :], part_refs[part], leave.at[part]
            )
        )
        outs[-1].start()
    for out in outs:
        out.wait()


def field_kernel(meta, *refs):
    (terms, tiles, low_bits, axes) = meta
    kernel_ref = refs[terms]
    outs = refs[terms + 1 : terms + 1 + tiles]
    (held,) = refs[terms + 1 + tiles :]
    total = functools.reduce(lambda a, b: a + b, [ref[...] for ref in refs[:terms]])
    depth = total.shape[0]
    rounded = []
    tall = [
        total[m * LANES : (m + 1) * LANES, :].T.reshape(GROUPS, VALUES, LANES)
        for m in range(depth // LANES)
    ]
    for j in range(GROUPS):
        for m in range(depth // LANES):
            rounded.append(tall[m][j])
    left = jnp.concatenate(rounded, axis=1).astype(jnp.bfloat16)
    real = jnp.dot(left, kernel_ref[0], preferred_element_type=F32)
    imag = jnp.dot(left, kernel_ref[1], preferred_element_type=F32)
    far = jnp.concatenate([real[0:4] - imag[4:8], imag[0:4] + real[4:8]], axis=0)
    width = far.shape[1] // tiles
    for t in range(tiles):
        held[t] = far[:, t * width : (t + 1) * width]
    me = lax.axis_index(axes) >> low_bits
    for t in range(tiles):
        outs[t][...] = held[me ^ t]


def body(
    axes,
    sizes,
    field_in,
    heading_in,
    launch_domain,
    hop_domain,
    hit_facet,
    path_phase,
    facet_polar,
    facet_azimuth,
    facet_tilt,
    surface_resistance,
    surface_reactance,
    kernel,
):
    domains, bins = sizes
    count = domains * bins
    phases = sum_phases(bits_of(count))
    me = lax.axis_index(axes)
    low = lax.axis_index(axes[1]) & 1
    tubes = field_in.shape[1]
    facets = facet_polar.shape[0]
    owned = kernel.shape[1]
    depth = owned // GROUPS
    blocks = tubes // LANES
    total = count * depth

    rows = facets // LANES
    half = rows // 2
    mine = jnp.stack(
        [facet_polar, facet_azimuth, facet_tilt, surface_resistance, surface_reactance], axis=0
    ).reshape(5, rows, LANES)
    near = lax.dynamic_slice_in_dim(mine, low * half, half, 1)
    far = lax.dynamic_slice_in_dim(mine, (1 - low) * half, half, 1)
    held = [near]
    bit = 0
    while bit < bits_of(domains):
        span = min(3, bits_of(domains) - bit)
        held = [
            piece if e == 0 else send(piece, (e << bit), axes[0], domains)
            for e in range(1 << span)
            for piece in held
        ]
        bit += span
    pieces = []
    for e, piece in enumerate(held):
        pieces += [piece, far if e == 0 else send(piece, 1, axes[1], bins)]

    domain = jnp.concatenate([launch_domain.reshape(1, tubes), hop_domain.reshape(BOUNCES - 1, tubes)])
    owner = domain * bins + hit_facet // owned
    within = hit_facet % owned
    place = place_of(owner ^ me, phases)
    hit_rows = (place * depth + within % depth).reshape(BOUNCES * tubes)
    hit_groups = (within // depth).reshape(BOUNCES, blocks, LANES)
    phase = path_phase.reshape(BOUNCES, blocks, LANES)

    parts = 1 << len(phases[0])
    copies = 1
    while copies < 8 and copies * 2 * total * LANES * 4 <= 16 * 2**20:
        copies *= 2
    meta = (tubes, len(pieces), half, bins, depth, phases, parts, copies, axes)
    *sums, exit_field = pl.pallas_call(
        functools.partial(trace_kernel, meta),
        out_shape=[jax.ShapeDtypeStruct((total // parts, LANES), F32)] * parts
        + [jax.ShapeDtypeStruct((8, tubes), F32)],
        in_specs=[SMEM, VMEM, VMEM, VMEM, VMEM] + [ANY] * len(pieces),
        out_specs=[ANY] * parts + [VMEM],
        scratch_shapes=[
            pltpu.VMEM((len(pieces), 5, half, LANES), F32),
            pltpu.VMEM((VALUES * half, LANES), F32),
            pltpu.VMEM((BOUNCES * tubes, LANES), F32),
            pltpu.VMEM((VALUES * blocks, LANES), F32),
            pltpu.VMEM((total, LANES), F32),
            pltpu.SemaphoreType.DMA((len(pieces),)),
            pltpu.SemaphoreType.DMA((parts,)),
        ]
        + [pltpu.VMEM((total, LANES), F32)] * copies,
        compiler_params=pltpu.CompilerParams(vmem_limit_bytes=60 * 2**20),
    )(hit_rows, hit_groups, phase, field_in, heading_in, *pieces)

    for n, phase_bits in enumerate(phases):
        terms = [sums[0]] + [
            send(sums[d], spread(d, phase_bits), axes, count) for d in range(1, len(sums))
        ]
        if n + 1 < len(phases):
            parts = 1 << len(phases[n + 1])
            size = terms[0].shape[0] // parts
            sums = [
                functools.reduce(lambda a, b: a + b, [t[p * size : (p + 1) * size] for t in terms])
                for p in range(parts)
            ]

    columns = kernel.shape[2]
    tiles = columns // LANES
    low_bits = bits_of(count) - bits_of(tiles)
    partial = pl.pallas_call(
        functools.partial(field_kernel, (len(terms), tiles, low_bits, axes)),
        out_shape=[jax.ShapeDtypeStruct((8, LANES), F32)] * tiles,
        in_specs=[VMEM] * (len(terms) + 1),
        out_specs=[VMEM] * tiles,
        scratch_shapes=[pltpu.VMEM((tiles, 8, LANES), F32)],
        compiler_params=pltpu.CompilerParams(vmem_limit_bytes=40 * 2**20),
    )(*terms, kernel)
    tile = functools.reduce(
        lambda a, b: a + b,
        [partial[0]] + [send(partial[e], e << low_bits, axes, count) for e in range(1, tiles)],
    )
    bit = 0
    while bit < low_bits:
        span = min(2, low_bits - bit)
        tile = functools.reduce(
            lambda a, b: a + b,
            [tile] + [send(tile, e << bit, axes, count) for e in range(1, 1 << span)],
        )
        bit += span
    width = columns // count
    far_field = lax.dynamic_slice_in_dim(tile, (me & ((1 << low_bits) - 1)) * width, width, 1)
    return far_field, exit_field


def solution(mesh):
    both = ("dom", "bin")
    in_specs = (
        P(None, both),
        P(None, both),
        P(both, None),
        P(None, both, None),
        P(None, both),
        P(None, both),
        P("dom"),
        P("dom"),
        P("dom"),
        P("dom"),
        P("dom"),
        P(None, both, None),
    )
    out_specs = (P(None, both), P(None, both))
    sizes = (mesh.shape["dom"], mesh.shape["bin"])
    return jax.shard_map(
        functools.partial(body, both, sizes),
        mesh=mesh,
        in_specs=in_specs,
        out_specs=out_specs,
        check_vma=False,
    )
```

```python
import functools

import jax
import jax.numpy as jnp
from jax import lax
from jax.experimental import pallas as pl
from jax.experimental.pallas import tpu as pltpu
from jax.sharding import PartitionSpec as P

BOUNCES = 4
MOST_COPIES = 8
SMALL = 4 * 2**20
LARGE = 60 * 2**20
CHUNKS = 8
LANES = 128
VALUES = 8
GROUPS = LANES // VALUES
VMEM = pl.BlockSpec(memory_space=pltpu.VMEM)
SMEM = pl.BlockSpec(memory_space=pltpu.SMEM)
ANY = pl.BlockSpec(memory_space=pl.ANY)
F32 = jnp.float32


def bits_of(count):
    assert count & (count - 1) == 0
    return count.bit_length() - 1


def sum_phases(bits):
    phases = [[0]]
    rest = list(range(1, bits))
    while rest:
        phases.append(rest[:2])
        rest = rest[2:]
    return phases


def spread(digit, phase):
    return sum(((digit >> place) & 1) << bit for place, bit in enumerate(phase))


def place_of(offset, phases):
    place = 0
    for phase in phases:
        for bit in reversed(phase):
            place = place * 2 + ((offset >> bit) & 1)
    return place


def send(value, mask, axes, count):
    return lax.ppermute(value, axes, [(i, i ^ mask) for i in range(count)])


def sine_cosine(angle):
    turns = jnp.floor(angle * 0.6366197723675814 + 0.5)
    rest = angle - turns * 1.5703125
    rest = rest - turns * 4.837512969970703e-4
    rest = rest - turns * 7.54978995489188e-8
    square = rest * rest
    sine = rest + rest * square * (
        -1.6666654611e-1 + square * (8.3321608736e-3 - square * 1.9515295891e-4)
    )
    cosine = 1.0 - 0.5 * square + square * square * (
        4.166664568298827e-2 + square * (-1.388731625493765e-3 + square * 2.443315711809948e-5)
    )
    quarter = turns.astype(jnp.int32)
    odd = (quarter & 1) == 1
    first = jnp.where(odd, cosine, sine)
    second = jnp.where(odd, sine, cosine)
    return (
        jnp.where((quarter & 2) == 2, -first, first),
        jnp.where(((quarter + 1) & 2) == 2, -second, second),
    )


def divide(top_real, top_imag, low_real, low_imag):
    scale = 1.0 / (low_real * low_real + low_imag * low_imag)
    return (
        (top_real * low_real + top_imag * low_imag) * scale,
        (top_imag * low_real - top_real * low_imag) * scale,
    )


def bounce_once(field, heading, facet, sine, cosine):
    real = [cosine * field[i] - sine * field[4 + i] for i in range(4)]
    imag = [sine * field[i] + cosine * field[4 + i] for i in range(4)]
    normal = facet[0:3]
    eta_real, eta_imag, tilt_cos, tilt_sin = facet[3:7]
    incidence = heading[0] * normal[0] + heading[1] * normal[1] + heading[2] * normal[2]
    slant = jnp.abs(incidence)
    te_real, te_imag = divide(slant - eta_real, -eta_imag, slant + eta_real, eta_imag)
    tm_real, tm_imag = divide(
        eta_real * slant - 1.0, eta_imag * slant, eta_real * slant + 1.0, eta_imag * slant
    )
    out_real, out_imag = [None] * 4, [None] * 4
    for i in range(2):
        upper_real = tilt_cos * real[i] + tilt_sin * real[2 + i]
        lower_real = tilt_cos * real[2 + i] - tilt_sin * real[i]
        upper_imag = tilt_cos * imag[i] + tilt_sin * imag[2 + i]
        lower_imag = tilt_cos * imag[2 + i] - tilt_sin * imag[i]
        out_real[i] = te_real * upper_real - te_imag * upper_imag
        out_real[2 + i] = tm_real * lower_real - tm_imag * lower_imag
        out_imag[i] = te_real * upper_imag + te_imag * upper_real
        out_imag[2 + i] = tm_real * lower_imag + tm_imag * lower_real
    twice = 2.0 * incidence
    return out_real + out_imag, [heading[k] - twice * normal[k] for k in range(3)]


def pack_kernel(axes, rows, *refs):
    share, arrive = refs[5], refs[6]
    at = pl.multiple_of(lax.axis_index(axes[1]) * rows, rows)
    loads = [
        pltpu.make_async_copy(refs[k].at[pl.ds(at, rows), :], share.at[k], arrive.at[k])
        for k in range(5)
    ]
    for load in loads:
        load.start()
    for load in loads:
        load.wait()


def build_kernel(depth, *refs):
    out, frame = refs[-2], refs[-1]
    steps = depth // LANES
    base = 0
    for ref in refs[:-2]:
        pieces, _, rows, _ = ref.shape

        def build(n, carry, ref=ref, rows=rows, base=base):
            polar_sin, polar_cos = sine_cosine(ref[n, 0])
            azimuth_sin, azimuth_cos = sine_cosine(ref[n, 1])
            tilt_sin, tilt_cos = sine_cosine(ref[n, 2])
            values = [
                polar_sin * azimuth_cos,
                polar_sin * azimuth_sin,
                polar_cos,
                ref[n, 3],
                ref[n, 4],
                tilt_cos,
                tilt_sin,
                tilt_sin,
            ]
            for k in range(VALUES):
                frame[n % 2, k * rows : (k + 1) * rows, :] = values[k]
            for m in range(steps):
                tall = jnp.concatenate(
                    [
                        frame[n % 2, pl.ds(j * steps + m, VALUES, stride=rows), :]
                        for j in range(GROUPS)
                    ],
                    axis=0,
                )
                at = pl.multiple_of((base + n) * depth + m * LANES, LANES)
                out[pl.ds(at, LANES), :] = tall.T
            return carry

        lax.fori_loop(0, pieces, build, 0)
        base += pieces


def prepare_kernel(meta, launch, hop, hit, angle, field, heading, *refs):
    (owned, bins, depth, phases, axes) = meta
    rows, groups, sines, cosines, fields, headings, facets, angles = refs
    blocks = launch.shape[0]
    for k in range(blocks):
        lanes = slice(k * LANES, (k + 1) * LANES)
        facets[pl.ds(k, BOUNCES, stride=blocks), :] = hit[:, lanes]
        angles[pl.ds(k, BOUNCES, stride=blocks), :] = angle[:, lanes]
        fields[pl.ds(k, 8, stride=blocks), :] = field[:, lanes]
        headings[pl.ds(k, 3, stride=blocks), :] = heading[:, lanes]
    me = lax.axis_index(axes)
    for bounce in range(BOUNCES):
        at = slice(bounce * blocks, (bounce + 1) * blocks)
        domain = launch[...] if bounce == 0 else hop[(bounce - 1) * blocks : bounce * blocks, :]
        facet = facets[at, :]
        quarter = facet >> bits_of(owned)
        within = facet & (owned - 1)
        place = place_of((domain * bins + quarter) ^ me, phases)
        rows[at, :] = place * depth + (within & (depth - 1))
        groups[at, :] = within >> bits_of(depth)
        sine, cosine = sine_cosine(angles[at, :])
        sines[at, :] = sine
        cosines[at, :] = cosine


def trace_kernel(meta, *refs):
    (blocks, shares, parts, copies) = meta
    rows_ref, group_ref, sine_ref, cosine_ref, field_ref, heading_ref = refs[:6]
    share_refs = refs[6 : 6 + shares]
    part_refs = refs[6 + shares : 6 + shares + parts]
    exit_ref = refs[6 + shares + parts]
    scratch = refs[7 + shares + parts :]
    even, odd, even_held, odd_held, picked, fields, flat, arrive, leave = scratch[:9]
    sums = scratch[9:]
    total = sums[0].shape[0]
    count = BOUNCES * blocks

    loads = [
        pltpu.make_async_copy(
            share_refs[i],
            flat.at[pl.ds(i * (total // shares), total // shares), :],
            arrive.at[i],
        )
        for i in range(shares)
    ]
    for load in loads:
        load.start()

    clear = 64
    zeros = jnp.zeros((clear, LANES), F32)

    def wipe(i, carry):
        for ref in sums:
            ref[pl.ds(pl.multiple_of(i * clear, clear), clear), :] = zeros
        return carry

    lax.fori_loop(0, total // clear, wipe, 0)

    for load in loads:
        load.wait()

    def fetch(block, into):
        for u in range(LANES):
            into[u : u + 1, :] = flat[pl.ds(rows_ref[block * LANES + u], 1), :]

    def group_of(block):
        return jnp.broadcast_to(group_ref[pl.ds(block, 1), :], (VALUES, LANES))

    def pick(block, source):
        group = group_of(jnp.maximum(block, 0))
        tall = source[...].T.reshape(GROUPS, VALUES, LANES)
        left = [tall[j] for j in range(GROUPS)]
        level = 0
        while len(left) > 1:
            upper = ((group >> level) & 1) == 1
            left = [jnp.where(upper, left[2 * n + 1], left[2 * n]) for n in range(len(left) // 2)]
            level += 1
        picked[pl.ds(pl.multiple_of((block + 2) * VALUES, VALUES), VALUES), :] = left[0]

    def gather(i, carry):
        pick(2 * i - 2, even_held)
        pick(2 * i - 1, odd_held)
        fetch(2 * i, even)
        fetch(2 * i + 1, odd)
        even_held[...] = even[...]
        odd_held[...] = odd[...]
        return carry

    lax.fori_loop(0, count // 2, gather, 0)
    pick(count - 2, even_held)
    pick(count - 1, odd_held)

    field = [field_ref[c * blocks : (c + 1) * blocks, :] for c in range(8)]
    heading = [heading_ref[c * blocks : (c + 1) * blocks, :] for c in range(3)]
    for bounce in range(BOUNCES):
        facet = [
            picked[pl.ds((bounce * blocks + 2) * VALUES + c, blocks, stride=VALUES), :]
            for c in range(7)
        ]
        at = slice(bounce * blocks, (bounce + 1) * blocks)
        field, heading = bounce_once(field, heading, facet, sine_ref[at, :], cosine_ref[at, :])
        for c in range(VALUES):
            fields[bounce, c * blocks : (c + 1) * blocks, :] = field[c]
    for k in range(blocks):
        exit_ref[:, k * LANES : (k + 1) * LANES] = fields[
            BOUNCES - 1, pl.ds(k, VALUES, stride=blocks), :
        ]

    def widen(block, into):
        own = fields[block // blocks, pl.ds(block % blocks, VALUES, stride=blocks), :]
        group = group_of(block)
        tall = jnp.concatenate([jnp.where(group == j, own, 0.0) for j in range(GROUPS)], axis=0)
        into[...] = tall.T

    def add(block, source):
        for u in range(0, LANES, copies):
            fresh = []
            for c in range(copies):
                row = rows_ref[block * LANES + u + c]
                fresh.append((row, sums[c][pl.ds(row, 1), :] + source[u + c : u + c + 1, :]))
            for c in range(copies):
                sums[c][pl.ds(fresh[c][0], 1), :] = fresh[c][1]

    widen(0, even)

    def scatter(i, carry):
        widen(2 * i + 1, odd)
        add(2 * i, even)
        widen(jnp.minimum(2 * i + 2, count - 1), even)
        add(2 * i + 1, odd)
        return carry

    lax.fori_loop(0, count // 2, scatter, 0)

    size = total // parts
    outs = []
    for part in reversed(range(parts)):

        def merge(i, carry, part=part):
            at = pl.ds(pl.multiple_of(part * size + i * LANES, LANES), LANES)
            sums[0][at, :] = functools.reduce(lambda a, b: a + b, [ref[at, :] for ref in sums])
            return carry

        if copies > 1:
            lax.fori_loop(0, size // LANES, merge, 0)
        outs.append(
            pltpu.make_async_copy(
                sums[0].at[pl.ds(part * size, size), :], part_refs[part], leave.at[part]
            )
        )
        outs[-1].start()
    for out in outs:
        out.wait()


def field_kernel(meta, *refs):
    (terms, tiles, chunks) = meta
    kernel_ref, out, stream, arrive = refs[terms:]
    size = kernel_ref.shape[1] // chunks
    loads = [
        [
            pltpu.make_async_copy(
                kernel_ref.at[h, pl.ds(i * size, size), :],
                stream.at[h, pl.ds(i * size, size), :],
                arrive.at[i, h],
            )
            for h in range(2)
        ]
        for i in range(chunks)
    ]
    for pair in loads:
        for load in pair:
            load.start()
    total = functools.reduce(lambda a, b: a + b, [ref[...] for ref in refs[:terms]])
    depth = total.shape[0]
    rounded = []
    tall = [
        total[m * LANES : (m + 1) * LANES, :].T.reshape(GROUPS, VALUES, LANES)
        for m in range(depth // LANES)
    ]
    for j in range(GROUPS):
        for m in range(depth // LANES):
            rounded.append(tall[m][j])
    left = jnp.concatenate(rounded, axis=1).astype(jnp.bfloat16)
    real = jnp.zeros((VALUES, kernel_ref.shape[2]), F32)
    imag = real
    for i in range(chunks):
        for load in loads[i]:
            load.wait()
        piece = left[:, i * size : (i + 1) * size]
        real += jnp.dot(piece, stream[0, i * size : (i + 1) * size, :], preferred_element_type=F32)
        imag += jnp.dot(piece, stream[1, i * size : (i + 1) * size, :], preferred_element_type=F32)
    far = jnp.concatenate([real[0:4] - imag[4:8], imag[0:4] + real[4:8]], axis=0)
    count = out.shape[0]
    for i in range(count):
        tile = i * tiles // count
        out[i] = far[:, tile * LANES : (tile + 1) * LANES]


def body(
    axes,
    sizes,
    field_in,
    heading_in,
    launch_domain,
    hop_domain,
    hit_facet,
    path_phase,
    facet_polar,
    facet_azimuth,
    facet_tilt,
    surface_resistance,
    surface_reactance,
    kernel,
):
    domains, bins = sizes
    count = domains * bins
    phases = sum_phases(bits_of(count))
    me = lax.axis_index(axes)
    tubes = field_in.shape[1]
    facets = facet_polar.shape[0]
    owned = kernel.shape[1]
    depth = owned // GROUPS
    blocks = tubes // LANES
    total = count * depth

    lines = owned // LANES
    geometry = (facet_polar, facet_azimuth, facet_tilt, surface_resistance, surface_reactance)
    share = pl.pallas_call(
        functools.partial(pack_kernel, axes, lines),
        out_shape=jax.ShapeDtypeStruct((5, lines, LANES), F32),
        in_specs=[ANY] * 5,
        out_specs=VMEM,
        scratch_shapes=[pltpu.SemaphoreType.DMA((5,))],
        compiler_params=pltpu.CompilerParams(vmem_limit_bytes=LARGE),
    )(*[value.reshape(facets // LANES, LANES) for value in geometry])
    held = [share[None]]
    for phase_bits in reversed(phases[1:]):
        mine = held[0] if len(held) == 1 else jnp.concatenate(held)
        held = [mine] + [
            send(mine, spread(d, phase_bits), axes, count) for d in range(1, 1 << len(phase_bits))
        ]
    parts = 1 << len(phases[0])
    mine = pl.pallas_call(
        functools.partial(build_kernel, depth),
        out_shape=jax.ShapeDtypeStruct((total // parts, LANES), F32),
        in_specs=[VMEM] * len(held),
        out_specs=VMEM,
        scratch_shapes=[pltpu.VMEM((2, VALUES * lines, LANES), F32)],
        compiler_params=pltpu.CompilerParams(vmem_limit_bytes=SMALL + 8 * LANES * total),
    )(*held)
    tables = [mine] + [send(mine, spread(d, phases[0]), axes, count) for d in range(1, parts)]

    rows = BOUNCES * blocks
    whole = jax.ShapeDtypeStruct((rows, LANES), F32)
    marks = jax.ShapeDtypeStruct((rows, LANES), jnp.int32)
    hit_rows, *prepared = pl.pallas_call(
        functools.partial(prepare_kernel, (owned, bins, depth, phases, axes)),
        out_shape=[
            marks,
            marks,
            whole,
            whole,
            jax.ShapeDtypeStruct((8 * blocks, LANES), F32),
            jax.ShapeDtypeStruct((3 * blocks, LANES), F32),
        ],
        in_specs=[VMEM] * 6,
        out_specs=[VMEM] * 6,
        scratch_shapes=[pltpu.VMEM((rows, LANES), jnp.int32), pltpu.VMEM((rows, LANES), F32)],
        compiler_params=pltpu.CompilerParams(vmem_limit_bytes=LARGE),
    )(
        launch_domain.reshape(blocks, LANES),
        hop_domain.reshape((BOUNCES - 1) * blocks, LANES),
        hit_facet,
        path_phase,
        field_in,
        heading_in,
    )

    copies = 1
    while copies < MOST_COPIES and copies * 2 * total * LANES * 4 <= 16 * 2**20:
        copies *= 2
    meta = (blocks, len(tables), parts, copies)
    buffers = [
        ((LANES, LANES), F32),
        ((LANES, LANES), F32),
        ((LANES, LANES), F32),
        ((LANES, LANES), F32),
        ((VALUES * (rows + 2), LANES), F32),
        ((BOUNCES, VALUES * blocks, LANES), F32),
        ((total, LANES), F32),
    ]
    sum_buffers = [((total, LANES), F32)] * copies
    *sums, exit_field = pl.pallas_call(
        functools.partial(trace_kernel, meta),
        out_shape=[jax.ShapeDtypeStruct((total // parts, LANES), F32)] * parts
        + [jax.ShapeDtypeStruct((8, tubes), F32)],
        in_specs=[SMEM] + [VMEM] * 5 + [ANY] * len(tables),
        out_specs=[ANY] * parts + [VMEM],
        scratch_shapes=[pltpu.VMEM(*buffer) for buffer in buffers]
        + [
            pltpu.SemaphoreType.DMA((len(tables),)),
            pltpu.SemaphoreType.DMA((parts,)),
        ]
        + [pltpu.VMEM(*buffer) for buffer in sum_buffers],
        compiler_params=pltpu.CompilerParams(vmem_limit_bytes=LARGE),
    )(hit_rows.reshape(rows * LANES), *prepared, *tables)

    for n, phase_bits in enumerate(phases):
        terms = [sums[0]] + [
            send(sums[d], spread(d, phase_bits), axes, count) for d in range(1, len(sums))
        ]
        if n + 1 < len(phases):
            parts = 1 << len(phases[n + 1])
            size = terms[0].shape[0] // parts
            sums = [
                functools.reduce(lambda a, b: a + b, [t[p * size : (p + 1) * size] for t in terms])
                for p in range(parts)
            ]

    columns = kernel.shape[2]
    tiles = columns // LANES
    partial = pl.pallas_call(
        functools.partial(field_kernel, (len(terms), tiles, CHUNKS)),
        out_shape=jax.ShapeDtypeStruct((count, 8, LANES), F32),
        in_specs=[VMEM] * len(terms) + [ANY],
        out_specs=VMEM,
        scratch_shapes=[
            pltpu.VMEM(kernel.shape, kernel.dtype),
            pltpu.SemaphoreType.DMA((CHUNKS, 2)),
        ],
        compiler_params=pltpu.CompilerParams(vmem_limit_bytes=LARGE),
    )(*terms, kernel)
    tile = jnp.sum(lax.all_to_all(partial, axes, 0, 0, tiled=True), axis=0)
    width = columns // count
    far_field = lax.dynamic_slice_in_dim(tile, (me & (count // tiles - 1)) * width, width, 1)
    return far_field, exit_field


def solution(mesh):
    both = ("dom", "bin")
    in_specs = (
        P(None, both),
        P(None, both),
        P(both, None),
        P(None, both, None),
        P(None, both),
        P(None, both),
        P("dom"),
        P("dom"),
        P("dom"),
        P("dom"),
        P("dom"),
        P(None, both, None),
    )
    out_specs = (P(None, both), P(None, both))
    sizes = (mesh.shape["dom"], mesh.shape["bin"])
    return jax.shard_map(
        functools.partial(body, both, sizes),
        mesh=mesh,
        in_specs=in_specs,
        out_specs=out_specs,
        check_vma=False,
    )
```

```python
import functools

import jax
import jax.numpy as jnp
from jax import lax
from jax.experimental import pallas as pl
from jax.experimental.pallas import tpu as pltpu
from jax.sharding import PartitionSpec as P

BOUNCES = 4
MOST_COPIES = 8
SLOTS = 8
SMALL = 4 * 2**20
LARGE = 60 * 2**20
CHUNKS = 8
LANES = 128
VALUES = 8
GROUPS = LANES // VALUES
VMEM = pl.BlockSpec(memory_space=pltpu.VMEM)
ANY = pl.BlockSpec(memory_space=pl.ANY)
F32 = jnp.float32


def bits_of(count):
    assert count & (count - 1) == 0
    return count.bit_length() - 1


def sum_phases(bits):
    phases = [[0]]
    rest = list(range(1, bits))
    while rest:
        phases.append(rest[:2])
        rest = rest[2:]
    return phases


def spread(digit, phase):
    return sum(((digit >> place) & 1) << bit for place, bit in enumerate(phase))


def place_of(offset, phases):
    place = 0
    for phase in phases:
        for bit in reversed(phase):
            place = place * 2 + ((offset >> bit) & 1)
    return place


def send(value, mask, axes, count):
    return lax.ppermute(value, axes, [(i, i ^ mask) for i in range(count)])


def sine_cosine(angle):
    turns = jnp.floor(angle * 0.6366197723675814 + 0.5)
    rest = angle - turns * 1.5703125
    rest = rest - turns * 4.837512969970703e-4
    rest = rest - turns * 7.54978995489188e-8
    square = rest * rest
    sine = rest + rest * square * (
        -1.6666654611e-1 + square * (8.3321608736e-3 - square * 1.9515295891e-4)
    )
    cosine = 1.0 - 0.5 * square + square * square * (
        4.166664568298827e-2 + square * (-1.388731625493765e-3 + square * 2.443315711809948e-5)
    )
    quarter = turns.astype(jnp.int32)
    odd = (quarter & 1) == 1
    first = jnp.where(odd, cosine, sine)
    second = jnp.where(odd, sine, cosine)
    return (
        jnp.where((quarter & 2) == 2, -first, first),
        jnp.where(((quarter + 1) & 2) == 2, -second, second),
    )


def divide(top_real, top_imag, low_real, low_imag):
    scale = 1.0 / (low_real * low_real + low_imag * low_imag)
    return (
        (top_real * low_real + top_imag * low_imag) * scale,
        (top_imag * low_real - top_real * low_imag) * scale,
    )


def bounce_once(field, heading, facet, sine, cosine):
    real = [cosine * field[i] - sine * field[4 + i] for i in range(4)]
    imag = [sine * field[i] + cosine * field[4 + i] for i in range(4)]
    normal = facet[0:3]
    eta_real, eta_imag, tilt_cos, tilt_sin = facet[3:7]
    incidence = heading[0] * normal[0] + heading[1] * normal[1] + heading[2] * normal[2]
    slant = jnp.abs(incidence)
    te_real, te_imag = divide(slant - eta_real, -eta_imag, slant + eta_real, eta_imag)
    tm_real, tm_imag = divide(
        eta_real * slant - 1.0, eta_imag * slant, eta_real * slant + 1.0, eta_imag * slant
    )
    out_real, out_imag = [None] * 4, [None] * 4
    for i in range(2):
        upper_real = tilt_cos * real[i] + tilt_sin * real[2 + i]
        lower_real = tilt_cos * real[2 + i] - tilt_sin * real[i]
        upper_imag = tilt_cos * imag[i] + tilt_sin * imag[2 + i]
        lower_imag = tilt_cos * imag[2 + i] - tilt_sin * imag[i]
        out_real[i] = te_real * upper_real - te_imag * upper_imag
        out_real[2 + i] = tm_real * lower_real - tm_imag * lower_imag
        out_imag[i] = te_real * upper_imag + te_imag * upper_real
        out_imag[2 + i] = tm_real * lower_imag + tm_imag * lower_real
    twice = 2.0 * incidence
    return out_real + out_imag, [heading[k] - twice * normal[k] for k in range(3)]


def pack_kernel(axes, rows, *refs):
    share, arrive = refs[5], refs[6]
    at = pl.multiple_of(lax.axis_index(axes[1]) * rows, rows)
    loads = [
        pltpu.make_async_copy(refs[k].at[pl.ds(at, rows), :], share.at[k], arrive.at[k])
        for k in range(5)
    ]
    for load in loads:
        load.start()
    for load in loads:
        load.wait()


def build_kernel(depth, *refs):
    out, frame = refs[-2], refs[-1]
    steps = depth // LANES
    base = 0
    for ref in refs[:-2]:
        pieces, _, rows, _ = ref.shape

        def build(n, carry, ref=ref, rows=rows, base=base):
            polar_sin, polar_cos = sine_cosine(ref[n, 0])
            azimuth_sin, azimuth_cos = sine_cosine(ref[n, 1])
            tilt_sin, tilt_cos = sine_cosine(ref[n, 2])
            values = [
                polar_sin * azimuth_cos,
                polar_sin * azimuth_sin,
                polar_cos,
                ref[n, 3],
                ref[n, 4],
                tilt_cos,
                tilt_sin,
                tilt_sin,
            ]
            for k in range(VALUES):
                frame[n % 2, k * rows : (k + 1) * rows, :] = values[k]
            for m in range(steps):
                tall = jnp.concatenate(
                    [
                        frame[n % 2, pl.ds(j * steps + m, VALUES, stride=rows), :]
                        for j in range(GROUPS)
                    ],
                    axis=0,
                )
                at = pl.multiple_of((base + n) * depth + m * LANES, LANES)
                out[pl.ds(at, LANES), :] = tall.T
            return carry

        lax.fori_loop(0, pieces, build, 0)
        base += pieces


def prepare_kernel(meta, launch, hop, hit, angle, field, heading, *refs):
    (owned, bins, depth, phases, axes) = meta
    rows, groups, sines, cosines, fields, headings, facets, angles = refs
    blocks = launch.shape[0]
    for k in range(blocks):
        lanes = slice(k * LANES, (k + 1) * LANES)
        facets[pl.ds(k, BOUNCES, stride=blocks), :] = hit[:, lanes]
        angles[pl.ds(k, BOUNCES, stride=blocks), :] = angle[:, lanes]
        fields[pl.ds(k, 8, stride=blocks), :] = field[:, lanes]
        headings[pl.ds(k, 3, stride=blocks), :] = heading[:, lanes]
    me = lax.axis_index(axes)
    for bounce in range(BOUNCES):
        at = slice(bounce * blocks, (bounce + 1) * blocks)
        domain = launch[...] if bounce == 0 else hop[(bounce - 1) * blocks : bounce * blocks, :]
        facet = facets[at, :]
        quarter = facet >> bits_of(owned)
        within = facet & (owned - 1)
        place = place_of((domain * bins + quarter) ^ me, phases)
        rows[at, :] = place * depth + (within & (depth - 1))
        groups[at, :] = within >> bits_of(depth)
        sine, cosine = sine_cosine(angles[at, :])
        sines[at, :] = sine
        cosines[at, :] = cosine


def trace_kernel(meta, *refs):
    (blocks, shares, parts, copies) = meta
    rows_ref, group_ref, sine_ref, cosine_ref, field_ref, heading_ref = refs[:6]
    share_refs = refs[6 : 6 + shares]
    part_refs = refs[6 + shares : 6 + shares + parts]
    exit_ref = refs[6 + shares + parts]
    scratch = refs[7 + shares + parts :]
    buffers = [scratch[0:2], scratch[2:4]]
    picked, fields, flat, arrive, leave, fill = scratch[4:10]
    slots = scratch[10 : 10 + SLOTS]
    sums = scratch[10 + SLOTS :]
    pairs = BOUNCES * blocks // 2
    total = sums[0].shape[0]
    count = BOUNCES * blocks

    loads = [
        pltpu.make_async_copy(
            share_refs[i],
            flat.at[pl.ds(i * (total // shares), total // shares), :],
            arrive.at[i],
        )
        for i in range(shares)
    ]
    for load in loads:
        load.start()

    clear = 64
    zeros = jnp.zeros((clear, LANES), F32)

    def wipe(i, carry):
        for ref in sums:
            ref[pl.ds(pl.multiple_of(i * clear, clear), clear), :] = zeros
        return carry

    lax.fori_loop(0, total // clear, wipe, 0)

    def refill(pair, q):
        return pltpu.make_async_copy(rows_ref.at[pair], slots[q], fill.at[q])

    for q in range(SLOTS):
        refill(q, q).start()
    for load in loads:
        load.wait()

    def fetch(slot, first, into):
        for u in range(LANES):
            into[u : u + 1, :] = flat[pl.ds(slot[0, first + u], 1), :]

    def group_of(block):
        return jnp.broadcast_to(group_ref[pl.ds(block, 1), :], (VALUES, LANES))

    def pick(block, source):
        group = group_of(jnp.maximum(block, 0))
        tall = source[...].T.reshape(GROUPS, VALUES, LANES)
        left = [tall[j] for j in range(GROUPS)]
        level = 0
        while len(left) > 1:
            upper = ((group >> level) & 1) == 1
            left = [jnp.where(upper, left[2 * n + 1], left[2 * n]) for n in range(len(left) // 2)]
            level += 1
        picked[pl.ds(pl.multiple_of((block + 2) * VALUES, VALUES), VALUES), :] = left[0]

    def gather(i, carry):
        for q in range(SLOTS):
            pair = i * SLOTS + q
            before, now = buffers[(q + 1) % 2], buffers[q % 2]
            refill(pair, q).wait()
            for n in range(2):
                pick(2 * pair - 2 + n, before[n])
            for n in range(2):
                fetch(slots[q], n * LANES, now[n])
            refill(lax.rem(pair + SLOTS, pairs), q).start()
        return carry

    lax.fori_loop(0, pairs // SLOTS, gather, 0)
    for n in range(2):
        pick(count - 2 + n, buffers[1][n])

    field = [field_ref[c * blocks : (c + 1) * blocks, :] for c in range(8)]
    heading = [heading_ref[c * blocks : (c + 1) * blocks, :] for c in range(3)]
    for bounce in range(BOUNCES):
        facet = [
            picked[pl.ds((bounce * blocks + 2) * VALUES + c, blocks, stride=VALUES), :]
            for c in range(7)
        ]
        at = slice(bounce * blocks, (bounce + 1) * blocks)
        field, heading = bounce_once(field, heading, facet, sine_ref[at, :], cosine_ref[at, :])
        for c in range(VALUES):
            fields[bounce, c * blocks : (c + 1) * blocks, :] = field[c]
    for k in range(blocks):
        exit_ref[:, k * LANES : (k + 1) * LANES] = fields[
            BOUNCES - 1, pl.ds(k, VALUES, stride=blocks), :
        ]

    def widen(block, into):
        own = fields[block // blocks, pl.ds(block % blocks, VALUES, stride=blocks), :]
        group = group_of(block)
        tall = jnp.concatenate([jnp.where(group == j, own, 0.0) for j in range(GROUPS)], axis=0)
        into[...] = tall.T

    def add(slot, first, source):
        for u in range(0, LANES, copies):
            fresh = []
            for c in range(copies):
                row = slot[0, first + u + c]
                fresh.append((row, sums[c][pl.ds(row, 1), :] + source[u + c : u + c + 1, :]))
            for c in range(copies):
                sums[c][pl.ds(fresh[c][0], 1), :] = fresh[c][1]

    for n in range(2):
        widen(n, buffers[0][n])

    def scatter(i, carry):
        for q in range(SLOTS):
            pair = i * SLOTS + q
            now, after = buffers[q % 2], buffers[(q + 1) % 2]
            refill(pair, q).wait()
            for n in range(2):
                widen(jnp.minimum(2 * pair + 2, count - 2) + n, after[n])
            for n in range(2):
                add(slots[q], n * LANES, now[n])
            refill(lax.rem(pair + SLOTS, pairs), q).start()
        return carry

    lax.fori_loop(0, pairs // SLOTS, scatter, 0)
    for q in range(SLOTS):
        refill(q, q).wait()

    size = total // parts
    outs = []
    for part in reversed(range(parts)):

        def merge(i, carry, part=part):
            at = pl.ds(pl.multiple_of(part * size + i * LANES, LANES), LANES)
            sums[0][at, :] = functools.reduce(lambda a, b: a + b, [ref[at, :] for ref in sums])
            return carry

        if copies > 1:
            lax.fori_loop(0, size // LANES, merge, 0)
        outs.append(
            pltpu.make_async_copy(
                sums[0].at[pl.ds(part * size, size), :], part_refs[part], leave.at[part]
            )
        )
        outs[-1].start()
    for out in outs:
        out.wait()


def hold_kernel(source, out, arrive):
    size = source.shape[1] // CHUNKS
    loads = [
        pltpu.make_async_copy(
            source.at[h, pl.ds(i * size, size), :],
            out.at[h, pl.ds(i * size, size), :],
            arrive.at[i, h],
        )
        for i in range(CHUNKS)
        for h in range(2)
    ]
    for load in loads:
        load.start()
    for load in loads:
        load.wait()


def field_kernel(meta, *refs):
    (terms, tiles) = meta
    kernel_ref, out = refs[terms:]
    total = functools.reduce(lambda a, b: a + b, [ref[...] for ref in refs[:terms]])
    depth = total.shape[0]
    rounded = []
    tall = [
        total[m * LANES : (m + 1) * LANES, :].T.reshape(GROUPS, VALUES, LANES)
        for m in range(depth // LANES)
    ]
    for j in range(GROUPS):
        for m in range(depth // LANES):
            rounded.append(tall[m][j])
    left = jnp.concatenate(rounded, axis=1).astype(jnp.bfloat16)
    real = jnp.dot(left, kernel_ref[0], preferred_element_type=F32)
    imag = jnp.dot(left, kernel_ref[1], preferred_element_type=F32)
    far = jnp.concatenate([real[0:4] - imag[4:8], imag[0:4] + real[4:8]], axis=0)
    count = out.shape[0]
    for i in range(count):
        tile = i * tiles // count
        out[i] = far[:, tile * LANES : (tile + 1) * LANES]


def body(
    axes,
    sizes,
    field_in,
    heading_in,
    launch_domain,
    hop_domain,
    hit_facet,
    path_phase,
    facet_polar,
    facet_azimuth,
    facet_tilt,
    surface_resistance,
    surface_reactance,
    kernel,
):
    domains, bins = sizes
    count = domains * bins
    phases = sum_phases(bits_of(count))
    me = lax.axis_index(axes)
    tubes = field_in.shape[1]
    facets = facet_polar.shape[0]
    owned = kernel.shape[1]
    depth = owned // GROUPS
    blocks = tubes // LANES
    total = count * depth

    lines = owned // LANES
    geometry = (facet_polar, facet_azimuth, facet_tilt, surface_resistance, surface_reactance)
    share = pl.pallas_call(
        functools.partial(pack_kernel, axes, lines),
        out_shape=jax.ShapeDtypeStruct((5, lines, LANES), F32),
        in_specs=[ANY] * 5,
        out_specs=VMEM,
        scratch_shapes=[pltpu.SemaphoreType.DMA((5,))],
        compiler_params=pltpu.CompilerParams(vmem_limit_bytes=LARGE),
    )(*[value.reshape(facets // LANES, LANES) for value in geometry])
    held = [share[None]]
    for phase_bits in reversed(phases[1:]):
        mine = held[0] if len(held) == 1 else jnp.concatenate(held)
        held = [mine] + [
            send(mine, spread(d, phase_bits), axes, count) for d in range(1, 1 << len(phase_bits))
        ]
    parts = 1 << len(phases[0])
    mine = pl.pallas_call(
        functools.partial(build_kernel, depth),
        out_shape=jax.ShapeDtypeStruct((total // parts, LANES), F32),
        in_specs=[VMEM] * len(held),
        out_specs=VMEM,
        scratch_shapes=[pltpu.VMEM((2, VALUES * lines, LANES), F32)],
        compiler_params=pltpu.CompilerParams(vmem_limit_bytes=SMALL + 8 * LANES * total),
    )(*held)
    tables = [mine] + [send(mine, spread(d, phases[0]), axes, count) for d in range(1, parts)]

    rows = BOUNCES * blocks
    whole = jax.ShapeDtypeStruct((rows, LANES), F32)
    marks = jax.ShapeDtypeStruct((rows, LANES), jnp.int32)
    hit_rows, *prepared = pl.pallas_call(
        functools.partial(prepare_kernel, (owned, bins, depth, phases, axes)),
        out_shape=[
            marks,
            marks,
            whole,
            whole,
            jax.ShapeDtypeStruct((8 * blocks, LANES), F32),
            jax.ShapeDtypeStruct((3 * blocks, LANES), F32),
        ],
        in_specs=[VMEM] * 6,
        out_specs=[VMEM] * 6,
        scratch_shapes=[pltpu.VMEM((rows, LANES), jnp.int32), pltpu.VMEM((rows, LANES), F32)],
        compiler_params=pltpu.CompilerParams(vmem_limit_bytes=LARGE),
    )(
        launch_domain.reshape(blocks, LANES),
        hop_domain.reshape((BOUNCES - 1) * blocks, LANES),
        hit_facet,
        path_phase,
        field_in,
        heading_in,
    )

    copies = 1
    while copies < MOST_COPIES and copies * 2 * total * LANES * 4 <= 16 * 2**20:
        copies *= 2
    meta = (blocks, len(tables), parts, copies)
    buffers = [
        ((LANES, LANES), F32),
        ((LANES, LANES), F32),
        ((LANES, LANES), F32),
        ((LANES, LANES), F32),
        ((VALUES * (rows + 2), LANES), F32),
        ((BOUNCES, VALUES * blocks, LANES), F32),
        ((total, LANES), F32),
    ]
    sum_buffers = [((total, LANES), F32)] * copies
    *sums, exit_field = pl.pallas_call(
        functools.partial(trace_kernel, meta),
        out_shape=[jax.ShapeDtypeStruct((total // parts, LANES), F32)] * parts
        + [jax.ShapeDtypeStruct((8, tubes), F32)],
        in_specs=[ANY] + [VMEM] * 5 + [ANY] * len(tables),
        out_specs=[ANY] * parts + [VMEM],
        scratch_shapes=[pltpu.VMEM(*buffer) for buffer in buffers]
        + [
            pltpu.SemaphoreType.DMA((len(tables),)),
            pltpu.SemaphoreType.DMA((parts,)),
            pltpu.SemaphoreType.DMA((SLOTS,)),
        ]
        + [pltpu.SMEM((1, 2 * LANES), jnp.int32)] * SLOTS
        + [pltpu.VMEM(*buffer) for buffer in sum_buffers],
        compiler_params=pltpu.CompilerParams(vmem_limit_bytes=LARGE),
    )(hit_rows.reshape(rows // 2, 1, 2 * LANES), *prepared, *tables)

    later, *sums = lax.optimization_barrier((kernel, *sums))
    near = pl.pallas_call(
        hold_kernel,
        out_shape=jax.ShapeDtypeStruct(kernel.shape, kernel.dtype),
        in_specs=[ANY],
        out_specs=ANY,
        scratch_shapes=[pltpu.SemaphoreType.DMA((CHUNKS, 2))],
        compiler_params=pltpu.CompilerParams(vmem_limit_bytes=SMALL),
        cost_estimate=pl.CostEstimate(flops=0, bytes_accessed=4 * kernel.size, transcendentals=0),
    )(later)

    for n, phase_bits in enumerate(phases):
        terms = [sums[0]] + [
            send(sums[d], spread(d, phase_bits), axes, count) for d in range(1, len(sums))
        ]
        if n + 2 == len(phases):
            near, *terms = lax.optimization_barrier((near, *terms))
        if n + 1 < len(phases):
            parts = 1 << len(phases[n + 1])
            size = terms[0].shape[0] // parts
            sums = [
                functools.reduce(lambda a, b: a + b, [t[p * size : (p + 1) * size] for t in terms])
                for p in range(parts)
            ]

    columns = kernel.shape[2]
    tiles = columns // LANES
    partial = pl.pallas_call(
        functools.partial(field_kernel, (len(terms), tiles)),
        out_shape=jax.ShapeDtypeStruct((count, 8, LANES), F32),
        in_specs=[VMEM] * (len(terms) + 1),
        out_specs=VMEM,
        compiler_params=pltpu.CompilerParams(vmem_limit_bytes=2 * SMALL),
    )(*terms, near)
    tile = jnp.sum(lax.all_to_all(partial, axes, 0, 0, tiled=True), axis=0)
    width = columns // count
    far_field = lax.dynamic_slice_in_dim(tile, (me & (count // tiles - 1)) * width, width, 1)
    return far_field, exit_field


def solution(mesh):
    both = ("dom", "bin")
    in_specs = (
        P(None, both),
        P(None, both),
        P(both, None),
        P(None, both, None),
        P(None, both),
        P(None, both),
        P("dom"),
        P("dom"),
        P("dom"),
        P("dom"),
        P("dom"),
        P(None, both, None),
    )
    out_specs = (P(None, both), P(None, both))
    sizes = (mesh.shape["dom"], mesh.shape["bin"])
    return jax.shard_map(
        functools.partial(body, both, sizes),
        mesh=mesh,
        in_specs=in_specs,
        out_specs=out_specs,
        check_vma=False,
    )
```

```python
import functools

import jax
import jax.numpy as jnp
from jax import lax
from jax.experimental import pallas as pl
from jax.experimental.pallas import tpu as pltpu
from jax.sharding import PartitionSpec as P

BOUNCES = 4
MOST_COPIES = 8
SLOTS = 8
SMALL = 4 * 2**20
LARGE = 60 * 2**20
CHUNKS = 8
LANES = 128
VALUES = 8
GROUPS = LANES // VALUES
VMEM = pl.BlockSpec(memory_space=pltpu.VMEM)
ANY = pl.BlockSpec(memory_space=pl.ANY)
F32 = jnp.float32


def bits_of(count):
    assert count & (count - 1) == 0
    return count.bit_length() - 1


def sum_phases(bits):
    phases = [[0]]
    rest = list(range(1, bits))
    while rest:
        phases.append(rest[:2])
        rest = rest[2:]
    return phases


def spread(digit, phase):
    return sum(((digit >> place) & 1) << bit for place, bit in enumerate(phase))


def place_of(offset, phases):
    place = 0
    for phase in phases:
        for bit in reversed(phase):
            place = place * 2 + ((offset >> bit) & 1)
    return place


def send(value, mask, axes, count):
    return lax.ppermute(value, axes, [(i, i ^ mask) for i in range(count)])


def sine_cosine(angle):
    turns = jnp.floor(angle * 0.6366197723675814 + 0.5)
    rest = angle - turns * 1.5703125
    rest = rest - turns * 4.837512969970703e-4
    rest = rest - turns * 7.54978995489188e-8
    square = rest * rest
    sine = rest + rest * square * (
        -1.6666654611e-1 + square * (8.3321608736e-3 - square * 1.9515295891e-4)
    )
    cosine = 1.0 - 0.5 * square + square * square * (
        4.166664568298827e-2 + square * (-1.388731625493765e-3 + square * 2.443315711809948e-5)
    )
    quarter = turns.astype(jnp.int32)
    odd = (quarter & 1) == 1
    first = jnp.where(odd, cosine, sine)
    second = jnp.where(odd, sine, cosine)
    return (
        jnp.where((quarter & 2) == 2, -first, first),
        jnp.where(((quarter + 1) & 2) == 2, -second, second),
    )


def divide(top_real, top_imag, low_real, low_imag):
    scale = 1.0 / (low_real * low_real + low_imag * low_imag)
    return (
        (top_real * low_real + top_imag * low_imag) * scale,
        (top_imag * low_real - top_real * low_imag) * scale,
    )


def bounce_once(field, heading, facet, sine, cosine):
    real = [cosine * field[i] - sine * field[4 + i] for i in range(4)]
    imag = [sine * field[i] + cosine * field[4 + i] for i in range(4)]
    normal = facet[0:3]
    eta_real, eta_imag, tilt_cos, tilt_sin = facet[3:7]
    incidence = heading[0] * normal[0] + heading[1] * normal[1] + heading[2] * normal[2]
    slant = jnp.abs(incidence)
    te_real, te_imag = divide(slant - eta_real, -eta_imag, slant + eta_real, eta_imag)
    tm_real, tm_imag = divide(
        eta_real * slant - 1.0, eta_imag * slant, eta_real * slant + 1.0, eta_imag * slant
    )
    out_real, out_imag = [None] * 4, [None] * 4
    for i in range(2):
        upper_real = tilt_cos * real[i] + tilt_sin * real[2 + i]
        lower_real = tilt_cos * real[2 + i] - tilt_sin * real[i]
        upper_imag = tilt_cos * imag[i] + tilt_sin * imag[2 + i]
        lower_imag = tilt_cos * imag[2 + i] - tilt_sin * imag[i]
        out_real[i] = te_real * upper_real - te_imag * upper_imag
        out_real[2 + i] = tm_real * lower_real - tm_imag * lower_imag
        out_imag[i] = te_real * upper_imag + te_imag * upper_real
        out_imag[2 + i] = tm_real * lower_imag + tm_imag * lower_real
    twice = 2.0 * incidence
    return out_real + out_imag, [heading[k] - twice * normal[k] for k in range(3)]


def pack_kernel(axes, rows, *refs):
    share, arrive = refs[5], refs[6]
    at = pl.multiple_of(lax.axis_index(axes[1]) * rows, rows)
    loads = [
        pltpu.make_async_copy(refs[k].at[pl.ds(at, rows), :], share.at[k], arrive.at[k])
        for k in range(5)
    ]
    for load in loads:
        load.start()
    for load in loads:
        load.wait()


def build_kernel(depth, *refs):
    out, frame = refs[-2], refs[-1]
    steps = depth // LANES
    base = 0
    for ref in refs[:-2]:
        pieces, _, rows, _ = ref.shape

        def build(n, carry, ref=ref, rows=rows, base=base):
            polar_sin, polar_cos = sine_cosine(ref[n, 0])
            azimuth_sin, azimuth_cos = sine_cosine(ref[n, 1])
            tilt_sin, tilt_cos = sine_cosine(ref[n, 2])
            values = [
                polar_sin * azimuth_cos,
                polar_sin * azimuth_sin,
                polar_cos,
                ref[n, 3],
                ref[n, 4],
                tilt_cos,
                tilt_sin,
                tilt_sin,
            ]
            for k in range(VALUES):
                frame[n % 2, k * rows : (k + 1) * rows, :] = values[k]
            for m in range(steps):
                tall = jnp.concatenate(
                    [
                        frame[n % 2, pl.ds(j * steps + m, VALUES, stride=rows), :]
                        for j in range(GROUPS)
                    ],
                    axis=0,
                )
                at = pl.multiple_of((base + n) * depth + m * LANES, LANES)
                out[pl.ds(at, LANES), :] = tall.T
            return carry

        lax.fori_loop(0, pieces, build, 0)
        base += pieces


def prepare_kernel(meta, launch, hop, hit, angle, field, heading, *refs):
    (owned, bins, depth, phases, axes) = meta
    rows, groups, sines, cosines, fields, headings, facets, angles = refs
    blocks = launch.shape[0]
    for k in range(blocks):
        lanes = slice(k * LANES, (k + 1) * LANES)
        facets[pl.ds(k, BOUNCES, stride=blocks), :] = hit[:, lanes]
        angles[pl.ds(k, BOUNCES, stride=blocks), :] = angle[:, lanes]
        fields[pl.ds(k, 8, stride=blocks), :] = field[:, lanes]
        headings[pl.ds(k, 3, stride=blocks), :] = heading[:, lanes]
    me = lax.axis_index(axes)
    for bounce in range(BOUNCES):
        at = slice(bounce * blocks, (bounce + 1) * blocks)
        domain = launch[...] if bounce == 0 else hop[(bounce - 1) * blocks : bounce * blocks, :]
        facet = facets[at, :]
        quarter = facet >> bits_of(owned)
        within = facet & (owned - 1)
        place = place_of((domain * bins + quarter) ^ me, phases)
        rows[at, :] = place * depth + (within & (depth - 1))
        groups[at, :] = within >> bits_of(depth)
        sine, cosine = sine_cosine(angles[at, :])
        sines[at, :] = sine
        cosines[at, :] = cosine


def trace_kernel(meta, *refs):
    (blocks, shares, parts, copies) = meta
    rows_ref, *given = refs[:6]
    share_refs = refs[6 : 6 + shares]
    part_refs = refs[6 + shares : 6 + shares + parts]
    exit_ref = refs[6 + shares + parts]
    scratch = refs[7 + shares + parts :]
    buffers = [scratch[0:2], scratch[2:4]]
    picked, fields, flat, arrive, leave, fill = scratch[4:10]
    slots = scratch[10 : 10 + SLOTS]
    exit_held, entering, *inner = scratch[10 + SLOTS : 17 + SLOTS]
    group_ref, sine_ref, cosine_ref, field_ref, heading_ref = inner
    sums = scratch[17 + SLOTS :]
    pairs = BOUNCES * blocks // 2
    total = sums[0].shape[0]
    count = BOUNCES * blocks

    loads = [
        pltpu.make_async_copy(
            share_refs[i],
            flat.at[pl.ds(i * (total // shares), total // shares), :],
            arrive.at[i],
        )
        for i in range(shares)
    ]
    for load in loads:
        load.start()
    enters = [pltpu.make_async_copy(given[i], inner[i], entering.at[i]) for i in range(5)]
    for enter in enters:
        enter.start()
    for q in range(SLOTS):
        pltpu.make_async_copy(rows_ref.at[q], slots[q], fill.at[q]).start()

    clear = 64
    zeros = jnp.zeros((clear, LANES), F32)

    def wipe(i, carry):
        for ref in sums:
            ref[pl.ds(pl.multiple_of(i * clear, clear), clear), :] = zeros
        return carry

    lax.fori_loop(0, total // clear, wipe, 0)

    def refill(pair, q):
        return pltpu.make_async_copy(rows_ref.at[pair], slots[q], fill.at[q])

    for load in loads:
        load.wait()
    enters[0].wait()

    def fetch(slot, first, into):
        for u in range(LANES):
            into[u : u + 1, :] = flat[pl.ds(slot[0, first + u], 1), :]

    def group_of(block):
        return jnp.broadcast_to(group_ref[pl.ds(block, 1), :], (VALUES, LANES))

    def pick(block, source):
        group = group_of(jnp.maximum(block, 0))
        tall = source[...].T.reshape(GROUPS, VALUES, LANES)
        left = [tall[j] for j in range(GROUPS)]
        level = 0
        while len(left) > 1:
            upper = ((group >> level) & 1) == 1
            left = [jnp.where(upper, left[2 * n + 1], left[2 * n]) for n in range(len(left) // 2)]
            level += 1
        picked[pl.ds(pl.multiple_of((block + 2) * VALUES, VALUES), VALUES), :] = left[0]

    def gather(i, carry):
        for q in range(SLOTS):
            pair = i * SLOTS + q
            before, now = buffers[(q + 1) % 2], buffers[q % 2]
            refill(pair, q).wait()
            for n in range(2):
                pick(2 * pair - 2 + n, before[n])
            for n in range(2):
                fetch(slots[q], n * LANES, now[n])
            refill(lax.rem(pair + SLOTS, pairs), q).start()
        return carry

    lax.fori_loop(0, pairs // SLOTS, gather, 0)
    for n in range(2):
        pick(count - 2 + n, buffers[1][n])

    for enter in enters[1:]:
        enter.wait()
    field = [field_ref[c * blocks : (c + 1) * blocks, :] for c in range(8)]
    heading = [heading_ref[c * blocks : (c + 1) * blocks, :] for c in range(3)]
    for bounce in range(BOUNCES):
        facet = [
            picked[pl.ds((bounce * blocks + 2) * VALUES + c, blocks, stride=VALUES), :]
            for c in range(7)
        ]
        at = slice(bounce * blocks, (bounce + 1) * blocks)
        field, heading = bounce_once(field, heading, facet, sine_ref[at, :], cosine_ref[at, :])
        for c in range(VALUES):
            fields[bounce, c * blocks : (c + 1) * blocks, :] = field[c]
    for k in range(blocks):
        exit_held[:, k * LANES : (k + 1) * LANES] = fields[
            BOUNCES - 1, pl.ds(k, VALUES, stride=blocks), :
        ]
    leaving = pltpu.make_async_copy(exit_held, exit_ref, entering.at[5])
    leaving.start()

    def widen(block, into):
        own = fields[block // blocks, pl.ds(block % blocks, VALUES, stride=blocks), :]
        group = group_of(block)
        tall = jnp.concatenate([jnp.where(group == j, own, 0.0) for j in range(GROUPS)], axis=0)
        into[...] = tall.T

    def add(slot, first, source):
        for u in range(0, LANES, copies):
            at = [slot[0, first + u + c] for c in range(copies)]
            fresh = [sums[c][pl.ds(at[c], 1), :] for c in range(copies)]
            extra = [source[u + c : u + c + 1, :] for c in range(copies)]
            for c in range(copies):
                sums[c][pl.ds(at[c], 1), :] = fresh[c] + extra[c]

    for n in range(2):
        widen(n, buffers[0][n])

    def scatter(i, carry):
        for q in range(SLOTS):
            pair = i * SLOTS + q
            now, after = buffers[q % 2], buffers[(q + 1) % 2]
            refill(pair, q).wait()
            for n in range(2):
                widen(jnp.minimum(2 * pair + 2, count - 2) + n, after[n])
            for n in range(2):
                add(slots[q], n * LANES, now[n])
            refill(lax.rem(pair + SLOTS, pairs), q).start()
        return carry

    lax.fori_loop(0, pairs // SLOTS, scatter, 0)
    for q in range(SLOTS):
        refill(q, q).wait()

    size = total // parts
    outs = []
    for part in reversed(range(parts)):

        def merge(i, carry, part=part):
            at = pl.ds(pl.multiple_of(part * size + i * LANES, LANES), LANES)
            sums[0][at, :] = functools.reduce(lambda a, b: a + b, [ref[at, :] for ref in sums])
            return carry

        if copies > 1:
            lax.fori_loop(0, size // LANES, merge, 0)
        outs.append(
            pltpu.make_async_copy(
                sums[0].at[pl.ds(part * size, size), :], part_refs[part], leave.at[part]
            )
        )
        outs[-1].start()
    for out in outs:
        out.wait()
    leaving.wait()


def hold_kernel(source, out, arrive):
    size = source.shape[1] // CHUNKS
    loads = [
        pltpu.make_async_copy(
            source.at[h, pl.ds(i * size, size), :],
            out.at[h, pl.ds(i * size, size), :],
            arrive.at[i, h],
        )
        for i in range(CHUNKS)
        for h in range(2)
    ]
    for load in loads:
        load.start()
    for load in loads:
        load.wait()


def field_kernel(meta, *refs):
    (terms, tiles) = meta
    kernel_ref, out = refs[terms:]
    total = functools.reduce(lambda a, b: a + b, [ref[...] for ref in refs[:terms]])
    depth = total.shape[0]
    rounded = []
    tall = [
        total[m * LANES : (m + 1) * LANES, :].T.reshape(GROUPS, VALUES, LANES)
        for m in range(depth // LANES)
    ]
    for j in range(GROUPS):
        for m in range(depth // LANES):
            rounded.append(tall[m][j])
    left = jnp.concatenate(rounded, axis=1).astype(jnp.bfloat16)
    real = jnp.dot(left, kernel_ref[0], preferred_element_type=F32)
    imag = jnp.dot(left, kernel_ref[1], preferred_element_type=F32)
    far = jnp.concatenate([real[0:4] - imag[4:8], imag[0:4] + real[4:8]], axis=0)
    count = out.shape[0]
    for i in range(count):
        tile = i * tiles // count
        out[i] = far[:, tile * LANES : (tile + 1) * LANES]


def body(
    axes,
    sizes,
    field_in,
    heading_in,
    launch_domain,
    hop_domain,
    hit_facet,
    path_phase,
    facet_polar,
    facet_azimuth,
    facet_tilt,
    surface_resistance,
    surface_reactance,
    kernel,
):
    domains, bins = sizes
    count = domains * bins
    phases = sum_phases(bits_of(count))
    me = lax.axis_index(axes)
    tubes = field_in.shape[1]
    facets = facet_polar.shape[0]
    owned = kernel.shape[1]
    depth = owned // GROUPS
    blocks = tubes // LANES
    total = count * depth

    lines = owned // LANES
    geometry = (facet_polar, facet_azimuth, facet_tilt, surface_resistance, surface_reactance)
    share = pl.pallas_call(
        functools.partial(pack_kernel, axes, lines),
        out_shape=jax.ShapeDtypeStruct((5, lines, LANES), F32),
        in_specs=[ANY] * 5,
        out_specs=VMEM,
        scratch_shapes=[pltpu.SemaphoreType.DMA((5,))],
        compiler_params=pltpu.CompilerParams(vmem_limit_bytes=LARGE),
    )(*[value.reshape(facets // LANES, LANES) for value in geometry])
    held = [share[None]]
    for phase_bits in reversed(phases[1:]):
        mine = held[0] if len(held) == 1 else jnp.concatenate(held)
        held = [mine] + [
            send(mine, spread(d, phase_bits), axes, count) for d in range(1, 1 << len(phase_bits))
        ]
    parts = 1 << len(phases[0])
    mine = pl.pallas_call(
        functools.partial(build_kernel, depth),
        out_shape=jax.ShapeDtypeStruct((total // parts, LANES), F32),
        in_specs=[VMEM] * len(held),
        out_specs=VMEM,
        scratch_shapes=[pltpu.VMEM((2, VALUES * lines, LANES), F32)],
        compiler_params=pltpu.CompilerParams(vmem_limit_bytes=SMALL + 8 * LANES * total),
    )(*held)
    tables = [mine] + [send(mine, spread(d, phases[0]), axes, count) for d in range(1, parts)]

    rows = BOUNCES * blocks
    whole = jax.ShapeDtypeStruct((rows, LANES), F32)
    marks = jax.ShapeDtypeStruct((rows, LANES), jnp.int32)
    hit_rows, *prepared = pl.pallas_call(
        functools.partial(prepare_kernel, (owned, bins, depth, phases, axes)),
        out_shape=[
            marks,
            marks,
            whole,
            whole,
            jax.ShapeDtypeStruct((8 * blocks, LANES), F32),
            jax.ShapeDtypeStruct((3 * blocks, LANES), F32),
        ],
        in_specs=[VMEM] * 6,
        out_specs=[VMEM] * 6,
        scratch_shapes=[pltpu.VMEM((rows, LANES), jnp.int32), pltpu.VMEM((rows, LANES), F32)],
        compiler_params=pltpu.CompilerParams(vmem_limit_bytes=LARGE),
    )(
        launch_domain.reshape(blocks, LANES),
        hop_domain.reshape((BOUNCES - 1) * blocks, LANES),
        hit_facet,
        path_phase,
        field_in,
        heading_in,
    )

    copies = 1
    while copies < MOST_COPIES and copies * 2 * total * LANES * 4 <= 32 * 2**20:
        copies *= 2
    meta = (blocks, len(tables), parts, copies)
    buffers = [
        ((LANES, LANES), F32),
        ((LANES, LANES), F32),
        ((LANES, LANES), F32),
        ((LANES, LANES), F32),
        ((VALUES * (rows + 2), LANES), F32),
        ((BOUNCES, VALUES * blocks, LANES), F32),
        ((total, LANES), F32),
    ]
    sum_buffers = [((total, LANES), F32)] * copies
    *sums, exit_field = pl.pallas_call(
        functools.partial(trace_kernel, meta),
        out_shape=[jax.ShapeDtypeStruct((total // parts, LANES), F32)] * parts
        + [jax.ShapeDtypeStruct((8, tubes), F32)],
        in_specs=[ANY] * (6 + len(tables)),
        out_specs=[ANY] * (parts + 1),
        scratch_shapes=[pltpu.VMEM(*buffer) for buffer in buffers]
        + [
            pltpu.SemaphoreType.DMA((len(tables),)),
            pltpu.SemaphoreType.DMA((parts,)),
            pltpu.SemaphoreType.DMA((SLOTS,)),
        ]
        + [pltpu.SMEM((1, 2 * LANES), jnp.int32)] * SLOTS
        + [pltpu.VMEM((8, tubes), F32), pltpu.SemaphoreType.DMA((6,))]
        + [pltpu.VMEM(value.shape, value.dtype) for value in prepared]
        + [pltpu.VMEM(*buffer) for buffer in sum_buffers],
        compiler_params=pltpu.CompilerParams(vmem_limit_bytes=LARGE),
    )(hit_rows.reshape(rows // 2, 1, 2 * LANES), *prepared, *tables)

    later, *sums = lax.optimization_barrier((kernel, *sums))
    near = pl.pallas_call(
        hold_kernel,
        out_shape=jax.ShapeDtypeStruct(kernel.shape, kernel.dtype),
        in_specs=[ANY],
        out_specs=ANY,
        scratch_shapes=[pltpu.SemaphoreType.DMA((CHUNKS, 2))],
        compiler_params=pltpu.CompilerParams(vmem_limit_bytes=SMALL),
        cost_estimate=pl.CostEstimate(flops=0, bytes_accessed=4 * kernel.size, transcendentals=0),
    )(later)

    for n, phase_bits in enumerate(phases):
        terms = [sums[0]] + [
            send(sums[d], spread(d, phase_bits), axes, count) for d in range(1, len(sums))
        ]
        if n + 2 == len(phases):
            near, *terms = lax.optimization_barrier((near, *terms))
        if n + 1 < len(phases):
            parts = 1 << len(phases[n + 1])
            size = terms[0].shape[0] // parts
            sums = [
                functools.reduce(lambda a, b: a + b, [t[p * size : (p + 1) * size] for t in terms])
                for p in range(parts)
            ]

    columns = kernel.shape[2]
    tiles = columns // LANES
    partial = pl.pallas_call(
        functools.partial(field_kernel, (len(terms), tiles)),
        out_shape=jax.ShapeDtypeStruct((count, 8, LANES), F32),
        in_specs=[VMEM] * (len(terms) + 1),
        out_specs=VMEM,
        compiler_params=pltpu.CompilerParams(vmem_limit_bytes=2 * SMALL),
    )(*terms, near)
    tile = jnp.sum(lax.all_to_all(partial, axes, 0, 0, tiled=True), axis=0)
    width = columns // count
    far_field = lax.dynamic_slice_in_dim(tile, (me & (count // tiles - 1)) * width, width, 1)
    return far_field, exit_field


def solution(mesh):
    both = ("dom", "bin")
    in_specs = (
        P(None, both),
        P(None, both),
        P(both, None),
        P(None, both, None),
        P(None, both),
        P(None, both),
        P("dom"),
        P("dom"),
        P("dom"),
        P("dom"),
        P("dom"),
        P(None, both, None),
    )
    out_specs = (P(None, both), P(None, both))
    sizes = (mesh.shape["dom"], mesh.shape["bin"])
    return jax.shard_map(
        functools.partial(body, both, sizes),
        mesh=mesh,
        in_specs=in_specs,
        out_specs=out_specs,
        check_vma=False,
    )
```

```python
import functools

import jax
import jax.numpy as jnp
from jax import lax
from jax.experimental import pallas as pl
from jax.experimental.pallas import tpu as pltpu
from jax.sharding import PartitionSpec as P

BOUNCES = 4
MOST_COPIES = 8
SLOTS = 8
MERGES = 4
SMALL = 4 * 2**20
LARGE = 60 * 2**20
CHUNKS = 8
LANES = 128
VALUES = 8
GROUPS = LANES // VALUES
VMEM = pl.BlockSpec(memory_space=pltpu.VMEM)
ANY = pl.BlockSpec(memory_space=pl.ANY)
F32 = jnp.float32


def bits_of(count):
    assert count & (count - 1) == 0
    return count.bit_length() - 1


def sum_phases(bits):
    phases = [[0]]
    rest = list(range(1, bits))
    while rest:
        phases.append(rest[:2])
        rest = rest[2:]
    return phases


def spread(digit, phase):
    return sum(((digit >> place) & 1) << bit for place, bit in enumerate(phase))


def place_of(offset, phases):
    place = 0
    for phase in phases:
        for bit in reversed(phase):
            place = place * 2 + ((offset >> bit) & 1)
    return place


def send(value, mask, axes, count):
    return lax.ppermute(value, axes, [(i, i ^ mask) for i in range(count)])


def sine_cosine(angle):
    turns = jnp.floor(angle * 0.6366197723675814 + 0.5)
    rest = angle - turns * 1.5703125
    rest = rest - turns * 4.837512969970703e-4
    rest = rest - turns * 7.54978995489188e-8
    square = rest * rest
    sine = rest + rest * square * (
        -1.6666654611e-1 + square * (8.3321608736e-3 - square * 1.9515295891e-4)
    )
    cosine = 1.0 - 0.5 * square + square * square * (
        4.166664568298827e-2 + square * (-1.388731625493765e-3 + square * 2.443315711809948e-5)
    )
    quarter = turns.astype(jnp.int32)
    odd = (quarter & 1) == 1
    first = jnp.where(odd, cosine, sine)
    second = jnp.where(odd, sine, cosine)
    return (
        jnp.where((quarter & 2) == 2, -first, first),
        jnp.where(((quarter + 1) & 2) == 2, -second, second),
    )


def divide(top_real, top_imag, low_real, low_imag):
    scale = 1.0 / (low_real * low_real + low_imag * low_imag)
    return (
        (top_real * low_real + top_imag * low_imag) * scale,
        (top_imag * low_real - top_real * low_imag) * scale,
    )


def bounce_once(field, heading, facet, sine, cosine):
    real = [cosine * field[i] - sine * field[4 + i] for i in range(4)]
    imag = [sine * field[i] + cosine * field[4 + i] for i in range(4)]
    normal = facet[0:3]
    eta_real, eta_imag, tilt_cos, tilt_sin = facet[3:7]
    incidence = heading[0] * normal[0] + heading[1] * normal[1] + heading[2] * normal[2]
    slant = jnp.abs(incidence)
    te_real, te_imag = divide(slant - eta_real, -eta_imag, slant + eta_real, eta_imag)
    tm_real, tm_imag = divide(
        eta_real * slant - 1.0, eta_imag * slant, eta_real * slant + 1.0, eta_imag * slant
    )
    out_real, out_imag = [None] * 4, [None] * 4
    for i in range(2):
        upper_real = tilt_cos * real[i] + tilt_sin * real[2 + i]
        lower_real = tilt_cos * real[2 + i] - tilt_sin * real[i]
        upper_imag = tilt_cos * imag[i] + tilt_sin * imag[2 + i]
        lower_imag = tilt_cos * imag[2 + i] - tilt_sin * imag[i]
        out_real[i] = te_real * upper_real - te_imag * upper_imag
        out_real[2 + i] = tm_real * lower_real - tm_imag * lower_imag
        out_imag[i] = te_real * upper_imag + te_imag * upper_real
        out_imag[2 + i] = tm_real * lower_imag + tm_imag * lower_real
    twice = 2.0 * incidence
    return out_real + out_imag, [heading[k] - twice * normal[k] for k in range(3)]


def pack_kernel(axes, rows, *refs):
    share, arrive = refs[5], refs[6]
    at = pl.multiple_of(lax.axis_index(axes[1]) * rows, rows)
    loads = [
        pltpu.make_async_copy(refs[k].at[pl.ds(at, rows), :], share.at[k], arrive.at[k])
        for k in range(5)
    ]
    for load in loads:
        load.start()
    for load in loads:
        load.wait()


def build_kernel(depth, *refs):
    out, frame = refs[-2], refs[-1]
    steps = depth // LANES
    base = 0
    for ref in refs[:-2]:
        pieces, _, rows, _ = ref.shape

        def build(n, carry, ref=ref, rows=rows, base=base):
            polar_sin, polar_cos = sine_cosine(ref[n, 0])
            azimuth_sin, azimuth_cos = sine_cosine(ref[n, 1])
            tilt_sin, tilt_cos = sine_cosine(ref[n, 2])
            values = [
                polar_sin * azimuth_cos,
                polar_sin * azimuth_sin,
                polar_cos,
                ref[n, 3],
                ref[n, 4],
                tilt_cos,
                tilt_sin,
                tilt_sin,
            ]
            for k in range(VALUES):
                frame[n % 2, k * rows : (k + 1) * rows, :] = values[k]
            for m in range(steps):
                tall = jnp.concatenate(
                    [
                        frame[n % 2, pl.ds(j * steps + m, VALUES, stride=rows), :]
                        for j in range(GROUPS)
                    ],
                    axis=0,
                )
                at = pl.multiple_of((base + n) * depth + m * LANES, LANES)
                out[pl.ds(at, LANES), :] = tall.T
            return carry

        lax.fori_loop(0, pieces, build, 0, unroll=min(pieces, 4))
        base += pieces


def prepare_kernel(meta, launch, hop, hit, angle, field, heading, *refs):
    (owned, bins, depth, phases, axes) = meta
    rows, groups, sines, cosines, fields, headings, facets, angles = refs
    blocks = launch.shape[0]
    for k in range(blocks):
        lanes = slice(k * LANES, (k + 1) * LANES)
        facets[pl.ds(k, BOUNCES, stride=blocks), :] = hit[:, lanes]
        angles[pl.ds(k, BOUNCES, stride=blocks), :] = angle[:, lanes]
        fields[pl.ds(k, 8, stride=blocks), :] = field[:, lanes]
        headings[pl.ds(k, 3, stride=blocks), :] = heading[:, lanes]
    me = lax.axis_index(axes)
    for bounce in range(BOUNCES):
        at = slice(bounce * blocks, (bounce + 1) * blocks)
        domain = launch[...] if bounce == 0 else hop[(bounce - 1) * blocks : bounce * blocks, :]
        facet = facets[at, :]
        quarter = facet >> bits_of(owned)
        within = facet & (owned - 1)
        place = place_of((domain * bins + quarter) ^ me, phases)
        rows[at, :] = place * depth + (within & (depth - 1))
        groups[at, :] = within >> bits_of(depth)
        sine, cosine = sine_cosine(angles[at, :])
        sines[at, :] = sine
        cosines[at, :] = cosine


def trace_kernel(meta, *refs):
    (blocks, shares, parts, copies) = meta
    rows_ref, *given = refs[:6]
    share_refs = refs[6 : 6 + shares]
    part_refs = refs[6 + shares : 6 + shares + parts]
    exit_ref = refs[6 + shares + parts]
    scratch = refs[7 + shares + parts :]
    buffers = [scratch[0:2], scratch[2:4]]
    picked, fields, flat, arrive, leave, fill = scratch[4:10]
    slots = scratch[10 : 10 + SLOTS]
    exit_held, entering, *inner = scratch[10 + SLOTS : 17 + SLOTS]
    group_ref, sine_ref, cosine_ref, field_ref, heading_ref = inner
    sums = scratch[17 + SLOTS :]
    pairs = BOUNCES * blocks // 2
    total = sums[0].shape[0]
    count = BOUNCES * blocks

    loads = [
        pltpu.make_async_copy(
            share_refs[i],
            flat.at[pl.ds(i * (total // shares), total // shares), :],
            arrive.at[i],
        )
        for i in range(shares)
    ]
    for load in loads:
        load.start()
    enters = [pltpu.make_async_copy(given[i], inner[i], entering.at[i]) for i in range(5)]
    for enter in enters:
        enter.start()
    for q in range(SLOTS):
        pltpu.make_async_copy(rows_ref.at[q], slots[q], fill.at[q]).start()

    clear = 64
    zeros = jnp.zeros((clear, LANES), F32)

    def wipe(i, carry):
        for ref in sums:
            ref[pl.ds(pl.multiple_of(i * clear, clear), clear), :] = zeros
        return carry

    lax.fori_loop(0, total // clear, wipe, 0)

    def refill(pair, q):
        return pltpu.make_async_copy(rows_ref.at[pair], slots[q], fill.at[q])

    for load in loads:
        load.wait()
    enters[0].wait()

    def fetch(slot, first, into):
        for u in range(LANES):
            into[u : u + 1, :] = flat[pl.ds(slot[0, first + u], 1), :]

    def group_of(block):
        return jnp.broadcast_to(group_ref[pl.ds(block, 1), :], (VALUES, LANES))

    def pick(block, source):
        group = group_of(jnp.maximum(block, 0))
        tall = source[...].T.reshape(GROUPS, VALUES, LANES)
        left = [tall[j] for j in range(GROUPS)]
        level = 0
        while len(left) > 1:
            upper = ((group >> level) & 1) == 1
            left = [jnp.where(upper, left[2 * n + 1], left[2 * n]) for n in range(len(left) // 2)]
            level += 1
        picked[pl.ds(pl.multiple_of((block + 2) * VALUES, VALUES), VALUES), :] = left[0]

    def gather(i, carry):
        for q in range(SLOTS):
            pair = i * SLOTS + q
            before, now = buffers[(q + 1) % 2], buffers[q % 2]
            refill(pair, q).wait()
            for n in range(2):
                pick(2 * pair - 2 + n, before[n])
            for n in range(2):
                fetch(slots[q], n * LANES, now[n])
            refill(lax.rem(pair + SLOTS, pairs), q).start()
        return carry

    lax.fori_loop(0, pairs // SLOTS, gather, 0)
    for n in range(2):
        pick(count - 2 + n, buffers[1][n])

    for enter in enters[1:]:
        enter.wait()
    field = [field_ref[c * blocks : (c + 1) * blocks, :] for c in range(8)]
    heading = [heading_ref[c * blocks : (c + 1) * blocks, :] for c in range(3)]
    for bounce in range(BOUNCES):
        facet = [
            picked[pl.ds((bounce * blocks + 2) * VALUES + c, blocks, stride=VALUES), :]
            for c in range(7)
        ]
        at = slice(bounce * blocks, (bounce + 1) * blocks)
        field, heading = bounce_once(field, heading, facet, sine_ref[at, :], cosine_ref[at, :])
        for c in range(VALUES):
            fields[bounce, c * blocks : (c + 1) * blocks, :] = field[c]
    for k in range(blocks):
        exit_held[:, k * LANES : (k + 1) * LANES] = fields[
            BOUNCES - 1, pl.ds(k, VALUES, stride=blocks), :
        ]
    leaving = pltpu.make_async_copy(exit_held, exit_ref, entering.at[5])
    leaving.start()

    def widen(block, into):
        own = fields[block // blocks, pl.ds(block % blocks, VALUES, stride=blocks), :]
        group = group_of(block)
        tall = jnp.concatenate([jnp.where(group == j, own, 0.0) for j in range(GROUPS)], axis=0)
        into[...] = tall.T

    def add(slot, first, source):
        for u in range(0, LANES, copies):
            at = [slot[0, first + u + c] for c in range(copies)]
            fresh = [sums[c][pl.ds(at[c], 1), :] for c in range(copies)]
            extra = [source[u + c : u + c + 1, :] for c in range(copies)]
            for c in range(copies):
                sums[c][pl.ds(at[c], 1), :] = fresh[c] + extra[c]

    for n in range(2):
        widen(n, buffers[0][n])

    def scatter(i, carry):
        for q in range(SLOTS):
            pair = i * SLOTS + q
            now, after = buffers[q % 2], buffers[(q + 1) % 2]
            refill(pair, q).wait()
            for n in range(2):
                widen(jnp.minimum(2 * pair + 2, count - 2) + n, after[n])
            for n in range(2):
                add(slots[q], n * LANES, now[n])
            refill(lax.rem(pair + SLOTS, pairs), q).start()
        return carry

    lax.fori_loop(0, pairs // SLOTS, scatter, 0)
    for q in range(SLOTS):
        refill(q, q).wait()

    size = total // parts
    chunk = size // MERGES
    outs = []
    for n, part in enumerate(reversed(range(parts))):
        for m in range(MERGES):
            begin = part * size + m * chunk

            def merge(i, carry, begin=begin):
                at = pl.ds(pl.multiple_of(begin + i * LANES, LANES), LANES)
                sums[0][at, :] = functools.reduce(lambda a, b: a + b, [ref[at, :] for ref in sums])
                return carry

            if copies > 1:
                lax.fori_loop(0, chunk // LANES, merge, 0)
            outs.append(
                pltpu.make_async_copy(
                    sums[0].at[pl.ds(begin, chunk), :],
                    part_refs[part].at[pl.ds(m * chunk, chunk), :],
                    leave.at[n * MERGES + m],
                )
            )
            outs[-1].start()
    for out in outs:
        out.wait()
    leaving.wait()


def hold_kernel(source, out, arrive):
    size = source.shape[1] // CHUNKS
    loads = [
        pltpu.make_async_copy(
            source.at[h, pl.ds(i * size, size), :],
            out.at[h, pl.ds(i * size, size), :],
            arrive.at[i, h],
        )
        for i in range(CHUNKS)
        for h in range(2)
    ]
    for load in loads:
        load.start()
    for load in loads:
        load.wait()


def field_kernel(meta, *refs):
    (terms, tiles) = meta
    kernel_ref, out = refs[terms:]
    total = functools.reduce(lambda a, b: a + b, [ref[...] for ref in refs[:terms]])
    depth = total.shape[0]
    rounded = []
    tall = [
        total[m * LANES : (m + 1) * LANES, :].T.reshape(GROUPS, VALUES, LANES)
        for m in range(depth // LANES)
    ]
    for j in range(GROUPS):
        for m in range(depth // LANES):
            rounded.append(tall[m][j])
    left = jnp.concatenate(rounded, axis=1).astype(jnp.bfloat16)
    real = jnp.dot(left, kernel_ref[0], preferred_element_type=F32)
    imag = jnp.dot(left, kernel_ref[1], preferred_element_type=F32)
    far = jnp.concatenate([real[0:4] - imag[4:8], imag[0:4] + real[4:8]], axis=0)
    count = out.shape[0]
    for i in range(count):
        tile = i * tiles // count
        out[i] = far[:, tile * LANES : (tile + 1) * LANES]


def body(
    axes,
    sizes,
    field_in,
    heading_in,
    launch_domain,
    hop_domain,
    hit_facet,
    path_phase,
    facet_polar,
    facet_azimuth,
    facet_tilt,
    surface_resistance,
    surface_reactance,
    kernel,
):
    domains, bins = sizes
    count = domains * bins
    phases = sum_phases(bits_of(count))
    me = lax.axis_index(axes)
    tubes = field_in.shape[1]
    facets = facet_polar.shape[0]
    owned = kernel.shape[1]
    depth = owned // GROUPS
    blocks = tubes // LANES
    total = count * depth

    lines = owned // LANES
    geometry = (facet_polar, facet_azimuth, facet_tilt, surface_resistance, surface_reactance)
    share = pl.pallas_call(
        functools.partial(pack_kernel, axes, lines),
        out_shape=jax.ShapeDtypeStruct((5, lines, LANES), F32),
        in_specs=[ANY] * 5,
        out_specs=VMEM,
        scratch_shapes=[pltpu.SemaphoreType.DMA((5,))],
        compiler_params=pltpu.CompilerParams(vmem_limit_bytes=LARGE),
    )(*[value.reshape(facets // LANES, LANES) for value in geometry])
    held = [share[None]]
    for phase_bits in reversed(phases[1:]):
        mine = held[0] if len(held) == 1 else jnp.concatenate(held)
        held = [mine] + [
            send(mine, spread(d, phase_bits), axes, count) for d in range(1, 1 << len(phase_bits))
        ]
    parts = 1 << len(phases[0])
    mine = pl.pallas_call(
        functools.partial(build_kernel, depth),
        out_shape=jax.ShapeDtypeStruct((total // parts, LANES), F32),
        in_specs=[VMEM] * len(held),
        out_specs=VMEM,
        scratch_shapes=[pltpu.VMEM((2, VALUES * lines, LANES), F32)],
        compiler_params=pltpu.CompilerParams(vmem_limit_bytes=SMALL + 8 * LANES * total),
    )(*held)
    tables = [mine] + [send(mine, spread(d, phases[0]), axes, count) for d in range(1, parts)]

    rows = BOUNCES * blocks
    whole = jax.ShapeDtypeStruct((rows, LANES), F32)
    marks = jax.ShapeDtypeStruct((rows, LANES), jnp.int32)
    hit_rows, *prepared = pl.pallas_call(
        functools.partial(prepare_kernel, (owned, bins, depth, phases, axes)),
        out_shape=[
            marks,
            marks,
            whole,
            whole,
            jax.ShapeDtypeStruct((8 * blocks, LANES), F32),
            jax.ShapeDtypeStruct((3 * blocks, LANES), F32),
        ],
        in_specs=[VMEM] * 6,
        out_specs=[VMEM] * 6,
        scratch_shapes=[pltpu.VMEM((rows, LANES), jnp.int32), pltpu.VMEM((rows, LANES), F32)],
        compiler_params=pltpu.CompilerParams(vmem_limit_bytes=LARGE),
    )(
        launch_domain.reshape(blocks, LANES),
        hop_domain.reshape((BOUNCES - 1) * blocks, LANES),
        hit_facet,
        path_phase,
        field_in,
        heading_in,
    )

    copies = 1
    while copies < MOST_COPIES and copies * 2 * total * LANES * 4 <= 32 * 2**20:
        copies *= 2
    meta = (blocks, len(tables), parts, copies)
    buffers = [
        ((LANES, LANES), F32),
        ((LANES, LANES), F32),
        ((LANES, LANES), F32),
        ((LANES, LANES), F32),
        ((VALUES * (rows + 2), LANES), F32),
        ((BOUNCES, VALUES * blocks, LANES), F32),
        ((total, LANES), F32),
    ]
    sum_buffers = [((total, LANES), F32)] * copies
    *sums, exit_field = pl.pallas_call(
        functools.partial(trace_kernel, meta),
        out_shape=[jax.ShapeDtypeStruct((total // parts, LANES), F32)] * parts
        + [jax.ShapeDtypeStruct((8, tubes), F32)],
        in_specs=[ANY] * (6 + len(tables)),
        out_specs=[ANY] * (parts + 1),
        scratch_shapes=[pltpu.VMEM(*buffer) for buffer in buffers]
        + [
            pltpu.SemaphoreType.DMA((len(tables),)),
            pltpu.SemaphoreType.DMA((parts * MERGES,)),
            pltpu.SemaphoreType.DMA((SLOTS,)),
        ]
        + [pltpu.SMEM((1, 2 * LANES), jnp.int32)] * SLOTS
        + [pltpu.VMEM((8, tubes), F32), pltpu.SemaphoreType.DMA((6,))]
        + [pltpu.VMEM(value.shape, value.dtype) for value in prepared]
        + [pltpu.VMEM(*buffer) for buffer in sum_buffers],
        compiler_params=pltpu.CompilerParams(vmem_limit_bytes=LARGE),
    )(hit_rows.reshape(rows // 2, 1, 2 * LANES), *prepared, *tables)

    later, *sums = lax.optimization_barrier((kernel, *sums))
    near = pl.pallas_call(
        hold_kernel,
        out_shape=jax.ShapeDtypeStruct(kernel.shape, kernel.dtype),
        in_specs=[ANY],
        out_specs=ANY,
        scratch_shapes=[pltpu.SemaphoreType.DMA((CHUNKS, 2))],
        compiler_params=pltpu.CompilerParams(vmem_limit_bytes=SMALL),
        cost_estimate=pl.CostEstimate(flops=0, bytes_accessed=4 * kernel.size, transcendentals=0),
    )(later)

    for n, phase_bits in enumerate(phases):
        terms = [sums[0]] + [
            send(sums[d], spread(d, phase_bits), axes, count) for d in range(1, len(sums))
        ]
        if n + 2 == len(phases):
            near, *terms = lax.optimization_barrier((near, *terms))
        if n + 1 < len(phases):
            parts = 1 << len(phases[n + 1])
            size = terms[0].shape[0] // parts
            sums = [
                functools.reduce(lambda a, b: a + b, [t[p * size : (p + 1) * size] for t in terms])
                for p in range(parts)
            ]

    columns = kernel.shape[2]
    tiles = columns // LANES
    partial = pl.pallas_call(
        functools.partial(field_kernel, (len(terms), tiles)),
        out_shape=jax.ShapeDtypeStruct((count, 8, LANES), F32),
        in_specs=[VMEM] * (len(terms) + 1),
        out_specs=VMEM,
        compiler_params=pltpu.CompilerParams(vmem_limit_bytes=2 * SMALL),
    )(*terms, near)
    tile = jnp.sum(lax.all_to_all(partial, axes, 0, 0, tiled=True), axis=0)
    width = columns // count
    far_field = lax.dynamic_slice_in_dim(tile, (me & (count // tiles - 1)) * width, width, 1)
    return far_field, exit_field


def solution(mesh):
    both = ("dom", "bin")
    in_specs = (
        P(None, both),
        P(None, both),
        P(both, None),
        P(None, both, None),
        P(None, both),
        P(None, both),
        P("dom"),
        P("dom"),
        P("dom"),
        P("dom"),
        P("dom"),
        P(None, both, None),
    )
    out_specs = (P(None, both), P(None, both))
    sizes = (mesh.shape["dom"], mesh.shape["bin"])
    return jax.shard_map(
        functools.partial(body, both, sizes),
        mesh=mesh,
        in_specs=in_specs,
        out_specs=out_specs,
        check_vma=False,
    )
```

```python
import functools

import jax
import jax.numpy as jnp
from jax import lax
from jax.experimental import pallas as pl
from jax.experimental.pallas import tpu as pltpu
from jax.sharding import PartitionSpec as P

BOUNCES = 4
MOST_COPIES = 8
SLOTS = 8
MERGES = 4
SMALL = 4 * 2**20
LARGE = 60 * 2**20
CHUNKS = 8
LANES = 128
VALUES = 8
GROUPS = LANES // VALUES
VMEM = pl.BlockSpec(memory_space=pltpu.VMEM)
ANY = pl.BlockSpec(memory_space=pl.ANY)
F32 = jnp.float32


def bits_of(count):
    assert count & (count - 1) == 0
    return count.bit_length() - 1


def sum_phases(bits):
    phases = [[0]]
    rest = list(range(1, bits))
    while rest:
        phases.append(rest[:2])
        rest = rest[2:]
    return phases


def spread(digit, phase):
    return sum(((digit >> place) & 1) << bit for place, bit in enumerate(phase))


def place_of(offset, phases):
    place = 0
    for phase in phases:
        for bit in reversed(phase):
            place = place * 2 + ((offset >> bit) & 1)
    return place


def send(value, mask, axes, count):
    return lax.ppermute(value, axes, [(i, i ^ mask) for i in range(count)])


def sine_cosine(angle):
    turns = jnp.floor(angle * 0.6366197723675814 + 0.5)
    rest = angle - turns * 1.5703125
    rest = rest - turns * 4.837512969970703e-4
    rest = rest - turns * 7.54978995489188e-8
    square = rest * rest
    sine = rest + rest * square * (
        -1.6666654611e-1 + square * (8.3321608736e-3 - square * 1.9515295891e-4)
    )
    cosine = 1.0 - 0.5 * square + square * square * (
        4.166664568298827e-2 + square * (-1.388731625493765e-3 + square * 2.443315711809948e-5)
    )
    quarter = turns.astype(jnp.int32)
    odd = (quarter & 1) == 1
    first = jnp.where(odd, cosine, sine)
    second = jnp.where(odd, sine, cosine)
    return (
        jnp.where((quarter & 2) == 2, -first, first),
        jnp.where(((quarter + 1) & 2) == 2, -second, second),
    )


def divide(top_real, top_imag, low_real, low_imag):
    scale = 1.0 / (low_real * low_real + low_imag * low_imag)
    return (
        (top_real * low_real + top_imag * low_imag) * scale,
        (top_imag * low_real - top_real * low_imag) * scale,
    )


def bounce_once(field, heading, facet, sine, cosine):
    real = [cosine * field[i] - sine * field[4 + i] for i in range(4)]
    imag = [sine * field[i] + cosine * field[4 + i] for i in range(4)]
    normal = facet[0:3]
    eta_real, eta_imag, tilt_cos, tilt_sin = facet[3:7]
    incidence = heading[0] * normal[0] + heading[1] * normal[1] + heading[2] * normal[2]
    slant = jnp.abs(incidence)
    te_real, te_imag = divide(slant - eta_real, -eta_imag, slant + eta_real, eta_imag)
    tm_real, tm_imag = divide(
        eta_real * slant - 1.0, eta_imag * slant, eta_real * slant + 1.0, eta_imag * slant
    )
    out_real, out_imag = [None] * 4, [None] * 4
    for i in range(2):
        upper_real = tilt_cos * real[i] + tilt_sin * real[2 + i]
        lower_real = tilt_cos * real[2 + i] - tilt_sin * real[i]
        upper_imag = tilt_cos * imag[i] + tilt_sin * imag[2 + i]
        lower_imag = tilt_cos * imag[2 + i] - tilt_sin * imag[i]
        out_real[i] = te_real * upper_real - te_imag * upper_imag
        out_real[2 + i] = tm_real * lower_real - tm_imag * lower_imag
        out_imag[i] = te_real * upper_imag + te_imag * upper_real
        out_imag[2 + i] = tm_real * lower_imag + tm_imag * lower_real
    twice = 2.0 * incidence
    return out_real + out_imag, [heading[k] - twice * normal[k] for k in range(3)]


def pack_kernel(axes, rows, *refs):
    share, arrive = refs[5], refs[6]
    at = pl.multiple_of(lax.axis_index(axes[1]) * rows, rows)
    loads = [
        pltpu.make_async_copy(refs[k].at[pl.ds(at, rows), :], share.at[k], arrive.at[k])
        for k in range(5)
    ]
    for load in loads:
        load.start()
    for load in loads:
        load.wait()


def build_kernel(depth, *refs):
    out, frame = refs[-2], refs[-1]
    steps = depth // LANES
    base = 0
    for ref in refs[:-2]:
        pieces, _, rows, _ = ref.shape

        def build(n, carry, ref=ref, rows=rows, base=base):
            polar_sin, polar_cos = sine_cosine(ref[n, 0])
            azimuth_sin, azimuth_cos = sine_cosine(ref[n, 1])
            tilt_sin, tilt_cos = sine_cosine(ref[n, 2])
            values = [
                polar_sin * azimuth_cos,
                polar_sin * azimuth_sin,
                polar_cos,
                ref[n, 3],
                ref[n, 4],
                tilt_cos,
                tilt_sin,
                tilt_sin,
            ]
            for k in range(VALUES):
                frame[n % 2, k * rows : (k + 1) * rows, :] = values[k]
            for m in range(steps):
                tall = jnp.concatenate(
                    [
                        frame[n % 2, pl.ds(j * steps + m, VALUES, stride=rows), :]
                        for j in range(GROUPS)
                    ],
                    axis=0,
                )
                at = pl.multiple_of((base + n) * depth + m * LANES, LANES)
                out[pl.ds(at, LANES), :] = tall.T
            return carry

        lax.fori_loop(0, pieces, build, 0, unroll=min(pieces, 4))
        base += pieces


def prepare_kernel(meta, launch, hop, hit, angle, field, heading, *refs):
    (owned, bins, depth, phases, axes) = meta
    rows, groups, sines, cosines, fields, headings, facets, angles = refs
    blocks = launch.shape[0]
    for k in range(blocks):
        lanes = slice(k * LANES, (k + 1) * LANES)
        facets[pl.ds(k, BOUNCES, stride=blocks), :] = hit[:, lanes]
        angles[pl.ds(k, BOUNCES, stride=blocks), :] = angle[:, lanes]
        fields[pl.ds(k, 8, stride=blocks), :] = field[:, lanes]
        headings[pl.ds(k, 3, stride=blocks), :] = heading[:, lanes]
    me = lax.axis_index(axes)
    for bounce in range(BOUNCES):
        at = slice(bounce * blocks, (bounce + 1) * blocks)
        domain = launch[...] if bounce == 0 else hop[(bounce - 1) * blocks : bounce * blocks, :]
        facet = facets[at, :]
        quarter = facet >> bits_of(owned)
        within = facet & (owned - 1)
        place = place_of((domain * bins + quarter) ^ me, phases)
        rows[at, :] = place * depth + (within & (depth - 1))
        groups[at, :] = within >> bits_of(depth)
        sine, cosine = sine_cosine(angles[at, :])
        sines[at, :] = sine
        cosines[at, :] = cosine


def trace_kernel(meta, *refs):
    (blocks, shares, parts, copies) = meta
    rows_ref, *given = refs[:6]
    share_refs = refs[6 : 6 + shares]
    part_refs = refs[6 + shares : 6 + shares + parts]
    exit_ref = refs[6 + shares + parts]
    scratch = refs[7 + shares + parts :]
    buffers = [scratch[0:2], scratch[2:4]]
    picked, fields, flat, arrive, leave, fill = scratch[4:10]
    slots = scratch[10 : 10 + SLOTS]
    exit_held, entering, *inner = scratch[10 + SLOTS : 17 + SLOTS]
    group_ref, sine_ref, cosine_ref, field_ref, heading_ref = inner
    sums = scratch[17 + SLOTS :]
    pairs = BOUNCES * blocks // 2
    total = sums[0].shape[0]
    count = BOUNCES * blocks

    loads = [
        pltpu.make_async_copy(
            share_refs[i],
            flat.at[pl.ds(i * (total // shares), total // shares), :],
            arrive.at[i],
        )
        for i in range(shares)
    ]
    for load in loads:
        load.start()
    enters = [pltpu.make_async_copy(given[i], inner[i], entering.at[i]) for i in range(5)]
    for enter in enters:
        enter.start()
    for q in range(SLOTS):
        pltpu.make_async_copy(rows_ref.at[q], slots[q], fill.at[q]).start()

    clear = 64
    zeros = jnp.zeros((clear, LANES), F32)

    def wipe(i, carry):
        for ref in sums:
            ref[pl.ds(pl.multiple_of(i * clear, clear), clear), :] = zeros
        return carry

    lax.fori_loop(0, total // clear, wipe, 0, unroll=2)

    def refill(pair, q):
        return pltpu.make_async_copy(rows_ref.at[pair], slots[q], fill.at[q])

    for load in loads:
        load.wait()
    enters[0].wait()

    def fetch(slot, first, into):
        for u in range(LANES):
            into[u : u + 1, :] = flat[pl.ds(slot[0, first + u], 1), :]

    def group_of(block):
        return jnp.broadcast_to(group_ref[pl.ds(block, 1), :], (VALUES, LANES))

    def pick(block, source):
        group = group_of(jnp.maximum(block, 0))
        tall = source[...].T.reshape(GROUPS, VALUES, LANES)
        left = [tall[j] for j in range(GROUPS)]
        level = 0
        while len(left) > 1:
            upper = ((group >> level) & 1) == 1
            left = [jnp.where(upper, left[2 * n + 1], left[2 * n]) for n in range(len(left) // 2)]
            level += 1
        picked[pl.ds(pl.multiple_of((block + 2) * VALUES, VALUES), VALUES), :] = left[0]

    def gather(i, carry):
        for q in range(SLOTS):
            pair = i * SLOTS + q
            before, now = buffers[(q + 1) % 2], buffers[q % 2]
            refill(pair, q).wait()
            for n in range(2):
                pick(2 * pair - 2 + n, before[n])
            for n in range(2):
                fetch(slots[q], n * LANES, now[n])
            refill(lax.rem(pair + SLOTS, pairs), q).start()
        return carry

    lax.fori_loop(0, pairs // SLOTS, gather, 0)
    for n in range(2):
        pick(count - 2 + n, buffers[1][n])

    for enter in enters[1:]:
        enter.wait()
    field = [field_ref[c * blocks : (c + 1) * blocks, :] for c in range(8)]
    heading = [heading_ref[c * blocks : (c + 1) * blocks, :] for c in range(3)]
    for bounce in range(BOUNCES):
        facet = [
            picked[pl.ds((bounce * blocks + 2) * VALUES + c, blocks, stride=VALUES), :]
            for c in range(7)
        ]
        at = slice(bounce * blocks, (bounce + 1) * blocks)
        field, heading = bounce_once(field, heading, facet, sine_ref[at, :], cosine_ref[at, :])
        for c in range(VALUES):
            fields[bounce, c * blocks : (c + 1) * blocks, :] = field[c]
    for k in range(blocks):
        exit_held[:, k * LANES : (k + 1) * LANES] = fields[
            BOUNCES - 1, pl.ds(k, VALUES, stride=blocks), :
        ]
    leaving = pltpu.make_async_copy(exit_held, exit_ref, entering.at[5])
    leaving.start()

    def widen(block, into):
        own = fields[block // blocks, pl.ds(block % blocks, VALUES, stride=blocks), :]
        group = group_of(block)
        tall = jnp.concatenate([jnp.where(group == j, own, 0.0) for j in range(GROUPS)], axis=0)
        into[...] = tall.T

    def add(slot, first, source):
        for u in range(0, LANES, copies):
            at = [slot[0, first + u + c] for c in range(copies)]
            fresh = [sums[c][pl.ds(at[c], 1), :] for c in range(copies)]
            extra = [source[u + c : u + c + 1, :] for c in range(copies)]
            for c in range(copies):
                sums[c][pl.ds(at[c], 1), :] = fresh[c] + extra[c]

    for n in range(2):
        widen(n, buffers[0][n])

    def scatter(i, carry):
        for q in range(SLOTS):
            pair = i * SLOTS + q
            now, after = buffers[q % 2], buffers[(q + 1) % 2]
            refill(pair, q).wait()
            for n in range(2):
                widen(jnp.minimum(2 * pair + 2, count - 2) + n, after[n])
            for n in range(2):
                add(slots[q], n * LANES, now[n])
            refill(lax.rem(pair + SLOTS, pairs), q).start()
        return carry

    lax.fori_loop(0, pairs // SLOTS, scatter, 0)
    for q in range(SLOTS):
        refill(q, q).wait()

    size = total // parts
    chunk = size // MERGES
    outs = []
    for n, part in enumerate(reversed(range(parts))):
        for m in range(MERGES):
            begin = part * size + m * chunk

            def merge(i, carry, begin=begin):
                at = pl.ds(pl.multiple_of(begin + i * LANES, LANES), LANES)
                sums[0][at, :] = functools.reduce(lambda a, b: a + b, [ref[at, :] for ref in sums])
                return carry

            if copies > 1:
                lax.fori_loop(0, chunk // LANES, merge, 0, unroll=2)
            outs.append(
                pltpu.make_async_copy(
                    sums[0].at[pl.ds(begin, chunk), :],
                    part_refs[part].at[pl.ds(m * chunk, chunk), :],
                    leave.at[n * MERGES + m],
                )
            )
            outs[-1].start()
    for out in outs:
        out.wait()
    leaving.wait()


def hold_kernel(source, out, arrive):
    size = source.shape[1] // CHUNKS
    loads = [
        pltpu.make_async_copy(
            source.at[h, pl.ds(i * size, size), :],
            out.at[h, pl.ds(i * size, size), :],
            arrive.at[i, h],
        )
        for i in range(CHUNKS)
        for h in range(2)
    ]
    for load in loads:
        load.start()
    for load in loads:
        load.wait()


def field_kernel(meta, *refs):
    (terms, tiles) = meta
    kernel_ref, out = refs[terms:]
    total = functools.reduce(lambda a, b: a + b, [ref[...] for ref in refs[:terms]])
    depth = total.shape[0]
    rounded = []
    tall = [
        total[m * LANES : (m + 1) * LANES, :].T.reshape(GROUPS, VALUES, LANES)
        for m in range(depth // LANES)
    ]
    for j in range(GROUPS):
        for m in range(depth // LANES):
            rounded.append(tall[m][j])
    left = jnp.concatenate(rounded, axis=1).astype(jnp.bfloat16)
    real = jnp.dot(left, kernel_ref[0], preferred_element_type=F32)
    imag = jnp.dot(left, kernel_ref[1], preferred_element_type=F32)
    far = jnp.concatenate([real[0:4] - imag[4:8], imag[0:4] + real[4:8]], axis=0)
    count = out.shape[0]
    for i in range(count):
        tile = i * tiles // count
        out[i] = far[:, tile * LANES : (tile + 1) * LANES]


def body(
    axes,
    sizes,
    field_in,
    heading_in,
    launch_domain,
    hop_domain,
    hit_facet,
    path_phase,
    facet_polar,
    facet_azimuth,
    facet_tilt,
    surface_resistance,
    surface_reactance,
    kernel,
):
    domains, bins = sizes
    count = domains * bins
    phases = sum_phases(bits_of(count))
    me = lax.axis_index(axes)
    tubes = field_in.shape[1]
    facets = facet_polar.shape[0]
    owned = kernel.shape[1]
    depth = owned // GROUPS
    blocks = tubes // LANES
    total = count * depth

    lines = owned // LANES
    geometry = (facet_polar, facet_azimuth, facet_tilt, surface_resistance, surface_reactance)
    share = pl.pallas_call(
        functools.partial(pack_kernel, axes, lines),
        out_shape=jax.ShapeDtypeStruct((5, lines, LANES), F32),
        in_specs=[ANY] * 5,
        out_specs=VMEM,
        scratch_shapes=[pltpu.SemaphoreType.DMA((5,))],
        compiler_params=pltpu.CompilerParams(vmem_limit_bytes=LARGE),
    )(*[value.reshape(facets // LANES, LANES) for value in geometry])
    held = [share[None]]
    for phase_bits in reversed(phases[1:]):
        mine = held[0] if len(held) == 1 else jnp.concatenate(held)
        held = [mine] + [
            send(mine, spread(d, phase_bits), axes, count) for d in range(1, 1 << len(phase_bits))
        ]
    parts = 1 << len(phases[0])
    mine = pl.pallas_call(
        functools.partial(build_kernel, depth),
        out_shape=jax.ShapeDtypeStruct((total // parts, LANES), F32),
        in_specs=[VMEM] * len(held),
        out_specs=VMEM,
        scratch_shapes=[pltpu.VMEM((2, VALUES * lines, LANES), F32)],
        compiler_params=pltpu.CompilerParams(vmem_limit_bytes=SMALL + 8 * LANES * total),
    )(*held)
    tables = [mine] + [send(mine, spread(d, phases[0]), axes, count) for d in range(1, parts)]

    rows = BOUNCES * blocks
    whole = jax.ShapeDtypeStruct((rows, LANES), F32)
    marks = jax.ShapeDtypeStruct((rows, LANES), jnp.int32)
    hit_rows, *prepared = pl.pallas_call(
        functools.partial(prepare_kernel, (owned, bins, depth, phases, axes)),
        out_shape=[
            marks,
            marks,
            whole,
            whole,
            jax.ShapeDtypeStruct((8 * blocks, LANES), F32),
            jax.ShapeDtypeStruct((3 * blocks, LANES), F32),
        ],
        in_specs=[VMEM] * 6,
        out_specs=[VMEM] * 6,
        scratch_shapes=[pltpu.VMEM((rows, LANES), jnp.int32), pltpu.VMEM((rows, LANES), F32)],
        compiler_params=pltpu.CompilerParams(vmem_limit_bytes=LARGE),
    )(
        launch_domain.reshape(blocks, LANES),
        hop_domain.reshape((BOUNCES - 1) * blocks, LANES),
        hit_facet,
        path_phase,
        field_in,
        heading_in,
    )

    copies = 1
    while copies < MOST_COPIES and copies * 2 * total * LANES * 4 <= 32 * 2**20:
        copies *= 2
    meta = (blocks, len(tables), parts, copies)
    buffers = [
        ((LANES, LANES), F32),
        ((LANES, LANES), F32),
        ((LANES, LANES), F32),
        ((LANES, LANES), F32),
        ((VALUES * (rows + 2), LANES), F32),
        ((BOUNCES, VALUES * blocks, LANES), F32),
        ((total, LANES), F32),
    ]
    sum_buffers = [((total, LANES), F32)] * copies
    *sums, exit_field = pl.pallas_call(
        functools.partial(trace_kernel, meta),
        out_shape=[jax.ShapeDtypeStruct((total // parts, LANES), F32)] * parts
        + [jax.ShapeDtypeStruct((8, tubes), F32)],
        in_specs=[ANY] * (6 + len(tables)),
        out_specs=[ANY] * (parts + 1),
        scratch_shapes=[pltpu.VMEM(*buffer) for buffer in buffers]
        + [
            pltpu.SemaphoreType.DMA((len(tables),)),
            pltpu.SemaphoreType.DMA((parts * MERGES,)),
            pltpu.SemaphoreType.DMA((SLOTS,)),
        ]
        + [pltpu.SMEM((1, 2 * LANES), jnp.int32)] * SLOTS
        + [pltpu.VMEM((8, tubes), F32), pltpu.SemaphoreType.DMA((6,))]
        + [pltpu.VMEM(value.shape, value.dtype) for value in prepared]
        + [pltpu.VMEM(*buffer) for buffer in sum_buffers],
        compiler_params=pltpu.CompilerParams(vmem_limit_bytes=LARGE),
    )(hit_rows.reshape(rows // 2, 1, 2 * LANES), *prepared, *tables)

    later, *sums = lax.optimization_barrier((kernel, *sums))
    near = pl.pallas_call(
        hold_kernel,
        out_shape=jax.ShapeDtypeStruct(kernel.shape, kernel.dtype),
        in_specs=[ANY],
        out_specs=ANY,
        scratch_shapes=[pltpu.SemaphoreType.DMA((CHUNKS, 2))],
        compiler_params=pltpu.CompilerParams(vmem_limit_bytes=SMALL),
        cost_estimate=pl.CostEstimate(flops=0, bytes_accessed=4 * kernel.size, transcendentals=0),
    )(later)

    for n, phase_bits in enumerate(phases):
        terms = [sums[0]] + [
            send(sums[d], spread(d, phase_bits), axes, count) for d in range(1, len(sums))
        ]
        if n + 2 == len(phases):
            near, *terms = lax.optimization_barrier((near, *terms))
        if n + 1 < len(phases):
            parts = 1 << len(phases[n + 1])
            size = terms[0].shape[0] // parts
            sums = [
                functools.reduce(lambda a, b: a + b, [t[p * size : (p + 1) * size] for t in terms])
                for p in range(parts)
            ]

    columns = kernel.shape[2]
    tiles = columns // LANES
    partial = pl.pallas_call(
        functools.partial(field_kernel, (len(terms), tiles)),
        out_shape=jax.ShapeDtypeStruct((count, 8, LANES), F32),
        in_specs=[VMEM] * (len(terms) + 1),
        out_specs=VMEM,
        compiler_params=pltpu.CompilerParams(vmem_limit_bytes=2 * SMALL),
    )(*terms, near)
    tile = jnp.sum(lax.all_to_all(partial, axes, 0, 0, tiled=True), axis=0)
    width = columns // count
    far_field = lax.dynamic_slice_in_dim(tile, (me & (count // tiles - 1)) * width, width, 1)
    return far_field, exit_field


def solution(mesh):
    both = ("dom", "bin")
    in_specs = (
        P(None, both),
        P(None, both),
        P(both, None),
        P(None, both, None),
        P(None, both),
        P(None, both),
        P("dom"),
        P("dom"),
        P("dom"),
        P("dom"),
        P("dom"),
        P(None, both, None),
    )
    out_specs = (P(None, both), P(None, both))
    sizes = (mesh.shape["dom"], mesh.shape["bin"])
    return jax.shard_map(
        functools.partial(body, both, sizes),
        mesh=mesh,
        in_specs=in_specs,
        out_specs=out_specs,
        check_vma=False,
    )
```
